32 devices in a mesh: dp: 4 (over z), fsdp: 8 (over y, x, core).
Axes of the slice: x: 2, y: 2, z: 4, core: 2. Of those that a mesh axis runs over, the one named last changes fastest.
Arguments:
- inputs: bfloat16 [8, 1024, 1024], P('dp', 'fsdp'), may hold values from -6 to 6
- norm_in: bfloat16 [1024], P('fsdp'), may hold values from 0.099609375 to 1.8984375
- w_in: bfloat16 [1024, 3072], P('fsdp'), may hold values from -0.1875 to 0.1875
- taps: bfloat16 [3, 1024], P(None, 'fsdp'), may hold values from -3.5 to 3.5
- w_out: bfloat16 [1024, 1024], P('fsdp'), may hold values from -0.1875 to 0.1875
- norm_mid: bfloat16 [1024], P('fsdp'), may hold values from 0.099609375 to 1.8984375
- w_gate: bfloat16 [1024, 4608], P('fsdp'), may hold values from -0.1875 to 0.1875
- w_up: bfloat16 [1024, 4608], P('fsdp'), may hold values from -0.1875 to 0.1875
- w_down: bfloat16 [4608, 1024], P('fsdp'), may hold values from -0.09375 to 0.09375
- cotangent: bfloat16 [8, 1024, 1024], P('dp', 'fsdp'), may hold values from -6 to 6
Outputs:
- block_out: bfloat16 [8, 1024, 1024], P('dp', 'fsdp')
- grad_inputs: float32 [8, 1024, 1024], P('dp', 'fsdp')
- grad_norm_in: float32 [1024], P('fsdp')
- grad_w_in: float32 [1024, 3072], P('fsdp')
- grad_taps: float32 [3, 1024], P(None, 'fsdp')
- grad_w_out: float32 [1024, 1024], P('fsdp')
- grad_norm_mid: float32 [1024], P('fsdp')
- grad_w_gate: float32 [1024, 4608], P('fsdp')
- grad_w_up: float32 [1024, 4608], P('fsdp')
- grad_w_down: float32 [4608, 1024], P('fsdp')
The draws below stay inside these ranges and needn't reach their ends.
All inputs are finite; a program needn't handle non-finite values.
Results may differ from the reference program's by a relative error of at most 0.011.
Values may be sent and summed in bfloat16 or wider, within the bound.
No kernel may reach another device: no remote copies, remote signals or barrier semaphores. Data moves between devices by JAX's collectives and lax.ppermute only.
A program may use at most 320 MiB of HBM per device.

```python
import jax
import jax.numpy as jnp
from jax import lax

D = 1024
FF = 4608
KW = 3
SEQ = 1024
BATCH = 8


def steps_of(key, dims, split, low, largest):
    loudness, own = 1.0, jax.random.fold_in(key, 6)
    for axis_at, blocks in split:
        heights = jnp.exp(jax.random.uniform(jax.random.fold_in(own, axis_at), (blocks,), jnp.float32, low / len(split), largest / len(split)))
        loudness = loudness * jnp.repeat(heights, dims[axis_at] // blocks).reshape([-1 if axis == axis_at else 1 for axis in range(len(dims))])
    return loudness


def bell_draw(own_key, dims, spread, most, pieces=(), held_as=jnp.bfloat16):
    loudness = steps_of(own_key, dims, pieces, -0.22, 0.18) if pieces else 1.0
    array = jax.random.normal(own_key, dims, jnp.float32) * spread * loudness
    return jnp.minimum(jnp.maximum(array, -most), most).astype(held_as)


def setup_inputs(seed: int = 0) -> dict:
    streams_of = jax.random.split(jax.random.key(seed), 11)
    return {
        "inputs": bell_draw(streams_of[0], (BATCH, SEQ, D), 1.0, 6.0, ((0, 4), (1, 8))),
        "norm_in": jnp.clip(1.0 + 0.18 * jax.random.normal(streams_of[1], (D,), jnp.float32), 0.099609375, 1.8984375).astype(jnp.bfloat16),
        "w_in": bell_draw(streams_of[2], (D, 3 * D), D ** -0.5, 0.1875, ((0, 8),)),
        "taps": bell_draw(streams_of[3], (KW, D), KW ** -0.5, 3.5, ((1, 8),)),
        "w_out": bell_draw(streams_of[4], (D, D), D ** -0.5, 0.1875, ((0, 8),)),
        "norm_mid": jnp.clip(1.0 + 0.18 * jax.random.normal(streams_of[5], (D,), jnp.float32), 0.099609375, 1.8984375).astype(jnp.bfloat16),
        "w_gate": bell_draw(streams_of[6], (D, FF), D ** -0.5, 0.1875, ((0, 8),)),
        "w_up": bell_draw(streams_of[7], (D, FF), D ** -0.5, 0.1875, ((0, 8),)),
        "w_down": bell_draw(streams_of[8], (FF, D), FF ** -0.5, 0.09375, ((0, 8),)),
        "cotangent": bell_draw(streams_of[9], (BATCH, SEQ, D), 1.0, 6.0, ((0, 4), (1, 8))),
    }


epsilon = 1e-05

@jax.custom_vjp
def low(v):
    return lax.optimization_barrier(v.astype(jnp.bfloat16)).astype(jnp.float32)

@jax.custom_vjp
def low_back(v):
    return v

def low_keep(v):
    return (low(v), None)

def low_pass(kept, grad):
    return (grad,)

def back_keep(v):
    return (v, None)

def back_low(kept, grad):
    return (low(grad),)
low.defvjp(low_keep, low_pass)
low_back.defvjp(back_keep, back_low)

def product(left, right):
    return jnp.dot(left, right, precision=lax.Precision.HIGHEST, preferred_element_type=jnp.float32)

def rms_normed(values):
    return values * lax.rsqrt(lax.optimization_barrier(jnp.mean(values * values, axis=-1, keepdims=True)) + epsilon)

def forward(params, sequence):
    norm_in, w_in, taps, w_out, norm_mid, w_gate, w_up, w_down = params
    width = w_out.shape[0]
    length = sequence.shape[0]
    reach = taps.shape[0] - 1
    normed_in = low(rms_normed(sequence) * norm_in)
    projected = low_back(product(normed_in, w_in))
    gate_b = projected[:, :width]
    gate_c = projected[:, width:2 * width]
    values = projected[:, 2 * width:]
    mixed = low(gate_b * values)
    padded = jnp.pad(mixed, ((reach, 0), (0, 0)))
    convolved = jnp.zeros_like(mixed)
    for offset in range(reach + 1):
        convolved = convolved + taps[offset] * padded[offset:offset + length]
    convolved = low_back(convolved)
    gated = low(gate_c * convolved)
    middle = sequence + low_back(product(gated, w_out))
    normed_mid = low(rms_normed(middle) * norm_mid)
    gate_pre = low_back(product(normed_mid, w_gate))
    up_pre = low_back(product(normed_mid, w_up))
    activ = low(jax.nn.silu(gate_pre) * up_pre)
    return middle + product(activ, w_down)

def reference(inputs, norm_in, w_in, taps, w_out, norm_mid, w_gate, w_up, w_down, cotangent):
    params = (norm_in.astype(jnp.float32), w_in.astype(jnp.float32), taps.astype(jnp.float32), w_out.astype(jnp.float32), norm_mid.astype(jnp.float32), w_gate.astype(jnp.float32), w_up.astype(jnp.float32), w_down.astype(jnp.float32))

    def per_sequence(totals, entry_pair):
        sequence, grad_seq_out = entry_pair
        result, pullback = jax.vjp(forward, params, sequence.astype(jnp.float32))
        grads, grad_sequence = pullback(grad_seq_out.astype(jnp.float32))
        totals = jax.tree.map(jnp.add, totals, grads)
        return (totals, (result.astype(jnp.bfloat16), grad_sequence))
    start = jax.tree.map(jnp.zeros_like, params)
    totals, stacked = lax.scan(per_sequence, start, (inputs, cotangent))
    block_out, grad_inputs = stacked
    g_norm_in, g_w_in, g_taps, g_w_out, g_norm_mid, g_w_gate, g_w_up, g_w_down = totals
    return (block_out, grad_inputs, g_norm_in, g_w_in, g_taps, g_w_out, g_norm_mid, g_w_gate, g_w_up, g_w_down)
```

```python
import jax
import jax.numpy as jnp
from jax import lax
from jax.sharding import PartitionSpec as P

epsilon = 1e-05
bf16 = jnp.bfloat16
f32 = jnp.float32


def along(shard, axis, pairs):
    return lax.ppermute(shard, axis, pairs)


def flip(shard, bits):
    peers = lax.axis_size("fsdp")
    return along(shard, "fsdp", [(i, i ^ bits) for i in range(peers)])


def flip_by_core(shard, even_bits, odd_bits):
    peers = lax.axis_size("fsdp")
    return along(
        shard, "fsdp", [(i, i ^ (odd_bits if i & 1 else even_bits)) for i in range(peers)]
    )


def is_cube():
    return lax.axis_size("fsdp") == 8


def on_odd_core():
    return (lax.axis_index("fsdp") & 1) == 1


def gather_relative(shard):
    if not is_cube():
        whole = lax.all_gather(shard, "fsdp", axis=0)
        return [whole[j] for j in range(lax.axis_size("fsdp"))]
    from_x = flip(shard, 2)
    from_y = flip(shard, 4)
    from_core = flip(shard, 1)
    across = flip_by_core(jnp.where(on_odd_core(), from_y, from_x), 4, 2)
    return [
        shard,
        from_core,
        from_x,
        flip(from_x, 1),
        from_y,
        flip(from_y, 1),
        across,
        flip(across, 1),
    ]


def scatter_relative(parts):
    if not is_cube():
        return lax.psum_scatter(
            jnp.stack([part.astype(bf16) for part in parts]), "fsdp", scatter_dimension=0
        ).astype(f32)
    parts = [part.astype(bf16) for part in parts]
    far = flip(parts[7], 1)
    near = flip(jnp.stack([parts[1], parts[3], parts[5]]), 1)
    odd = on_odd_core()
    across = flip_by_core((parts[6].astype(f32) + far).astype(bf16), 2, 4).astype(f32)
    zero = jnp.zeros((), f32)
    to_x = parts[2].astype(f32) + near[1] + jnp.where(odd, across, zero)
    to_y = parts[4].astype(f32) + near[2] + jnp.where(odd, zero, across)
    got_x = flip(to_x.astype(bf16), 2)
    got_y = flip(to_y.astype(bf16), 4)
    return parts[0].astype(f32) + near[0] + got_x + got_y


def exchange(blocks):
    peers = lax.axis_size("fsdp")
    if not is_cube():
        return lax.all_to_all(blocks, "fsdp", 0, 0)
    me = lax.axis_index("fsdp")
    result = blocks
    for j in range(1, peers):
        block = lax.dynamic_index_in_dim(blocks, me ^ j, 0, keepdims=False)
        result = lax.dynamic_update_index_in_dim(result, flip(block, j), me ^ j, 0)
    return result


def relabel(columns):
    peers = lax.axis_size("fsdp")
    if not is_cube():
        return columns
    size = columns.shape[-1] // peers
    me = lax.axis_index("fsdp")
    blocks = [columns[..., k * size : (k + 1) * size] for k in range(peers)]
    for bit in (1, 2, 4):
        swap = (me & bit) != 0
        blocks = [jnp.where(swap, blocks[k ^ bit], blocks[k]) for k in range(peers)]
    return jnp.concatenate(blocks, axis=-1)


def sum_over_groups(term):
    groups = lax.axis_size("dp")
    term = term.astype(bf16)
    if groups != 4:
        return lax.psum(term, "dp").astype(f32)
    inner = (lax.axis_index("dp") == 1) | (lax.axis_index("dp") == 2)
    pair = (term.astype(f32) + along(term, "dp", [(0, 1), (3, 2)])).astype(bf16)
    total = (pair.astype(f32) + along(pair, "dp", [(1, 2), (2, 1)])).astype(bf16)
    return jnp.where(inner, total, along(total, "dp", [(1, 0), (2, 3)])).astype(f32)


def from_behind(shard, axis, by):
    peers = lax.axis_size(axis)
    pairs = [(i, i + by) for i in range(peers) if 0 <= i + by < peers]
    return lax.ppermute(shard, axis, pairs)


def inverse_rms(values):
    return lax.rsqrt(jnp.mean(values * values, axis=-1, keepdims=True) + epsilon)


def norm_back(values, scale, gain, incoming):
    normed = values * scale
    gain_grad = jnp.sum(incoming * normed, axis=0)
    weighted = incoming * gain
    projection = jnp.mean(weighted * normed, axis=-1, keepdims=True)
    return (scale * (weighted - normed * projection), gain_grad)


def times(left, right):
    return jnp.dot(left, right, preferred_element_type=f32)


def over_tokens(left, right):
    return lax.dot_general(left, right, (((0,), (0,)), ((), ())), preferred_element_type=f32)


def against_rows(left, right):
    return lax.dot_general(left, right, (((1,), (1,)), ((), ())), preferred_element_type=f32)


def per_device(inputs, norm_in, w_in, taps, w_out, norm_mid, w_gate, w_up, w_down, cotangent):
    micros, rows, width = inputs.shape
    peers = lax.axis_size("fsdp")
    reach = taps.shape[0] - 1
    owned = w_in.shape[0]
    hidden = w_down.shape[0]
    all_rows = micros * rows
    small_rows = 16

    small = jnp.concatenate([norm_in, norm_mid, taps.reshape(-1)])
    small = jnp.pad(small, (0, small_rows * width - small.shape[0])).reshape(small_rows, width)
    packed = jnp.concatenate(
        [w_in[:, :width], w_in[:, width : 2 * width], w_in[:, 2 * width :], small], axis=0
    )
    in_pieces = gather_relative(packed)
    full_in = [
        jnp.concatenate([piece[k * owned : (k + 1) * owned] for piece in in_pieces], axis=0)
        for k in range(3)
    ]
    count = owned * (reach + 3)
    smalls = relabel(
        jnp.concatenate(
            [piece[3 * owned].reshape(-1)[:count].reshape(reach + 3, owned) for piece in in_pieces],
            axis=1,
        )
    ).astype(f32)
    gain_in, gain_mid, tap_values = smalls[0], smalls[1], smalls[2:]
    full_out = jnp.concatenate(gather_relative(w_out), axis=0)

    gate_up = jnp.stack(
        [w_gate.reshape(owned, peers, hidden), w_up.reshape(owned, peers, hidden)]
    )
    gate_up = exchange(jnp.transpose(gate_up, (2, 0, 1, 3)))
    own_gate = gate_up[:, 0].reshape(width, hidden)
    own_up = gate_up[:, 1].reshape(width, hidden)

    grad_out = cotangent.reshape(all_rows, width)
    grad_out_all = jnp.concatenate(gather_relative(grad_out), axis=0)

    resid = inputs.reshape(all_rows, width).astype(f32)
    scale_in = inverse_rms(resid)
    normed_in = relabel((resid * scale_in * gain_in).astype(bf16))
    gate_b = times(normed_in, full_in[0])
    gate_c = times(normed_in, full_in[1])
    values = times(normed_in, full_in[2])
    mixed = (gate_b * values).astype(bf16).reshape(micros, rows, width)
    earlier = from_behind(mixed[:, rows - reach :], "fsdp", 1)
    extended = jnp.concatenate([earlier, mixed], axis=1).astype(f32)
    convolved = jnp.zeros((micros, rows, width), f32)
    for offset in range(reach + 1):
        convolved = convolved + tap_values[offset] * extended[:, offset : offset + rows]
    convolved = convolved.reshape(all_rows, width)
    gated = relabel((gate_c * convolved).astype(bf16))
    middle = resid + times(gated, full_out)
    scale_mid = inverse_rms(middle)
    normed_mid = (middle * scale_mid * gain_mid).astype(bf16)

    normed_all = jnp.concatenate(gather_relative(normed_mid), axis=0)
    gate_pre = times(normed_all, own_gate)
    up_pre = times(normed_all, own_up)
    sigmoid_gate = jax.nn.sigmoid(gate_pre)
    activ = (gate_pre * sigmoid_gate * up_pre).astype(bf16)
    grad_w_down = over_tokens(activ, grad_out_all)
    half = hidden // 2
    grad_w_down = jnp.concatenate(
        [sum_over_groups(grad_w_down[:half]), sum_over_groups(grad_w_down[half:])], axis=0
    )
    grad_activ = against_rows(grad_out_all, w_down)
    grad_gate = (
        grad_activ * up_pre * sigmoid_gate * (1.0 + gate_pre * (1.0 - sigmoid_gate))
    ).astype(bf16)
    grad_up = (grad_activ * gate_pre * sigmoid_gate).astype(bf16)
    grad_normed = (against_rows(grad_gate, own_gate) + against_rows(grad_up, own_up)).astype(bf16)
    grad_normed_mid = scatter_relative(
        [grad_normed[j * all_rows : (j + 1) * all_rows] for j in range(peers)]
    )
    final = times(activ, w_down).astype(bf16)
    final = scatter_relative([final[j * all_rows : (j + 1) * all_rows] for j in range(peers)])
    block_out = (middle + final).astype(bf16).reshape(micros, rows, width)

    def to_owner(left, right):
        total = sum_over_groups(over_tokens(left, right)).astype(bf16)
        mine = exchange(total.reshape(peers, owned, hidden))
        return jnp.transpose(mine, (1, 0, 2)).reshape(owned, peers * hidden).astype(f32)

    grad_w_gate = to_owner(normed_all, grad_gate)
    grad_w_up = to_owner(normed_all, grad_up)

    back_mid, gain_mid_grad = norm_back(middle, scale_mid, gain_mid, grad_normed_mid)
    grad_middle = grad_out.astype(f32) + back_mid
    grad_branch = grad_middle.astype(bf16)
    grad_gated = relabel(against_rows(grad_branch, full_out))
    grad_c = grad_gated * convolved
    grad_conv = (grad_gated * gate_c).astype(bf16).reshape(micros, rows, width)
    later = from_behind(grad_conv[:, :reach], "fsdp", -1)
    ext_grad = jnp.concatenate([grad_conv, later], axis=1).astype(f32)
    grad_mixed = jnp.zeros((micros, rows, width), f32)
    tap_terms = []
    for offset in range(reach + 1):
        grad_mixed = (
            grad_mixed + tap_values[offset] * ext_grad[:, reach - offset : reach - offset + rows]
        )
        tap_terms.append(
            jnp.sum(extended[:, offset : offset + rows] * ext_grad[:, :rows], axis=(0, 1))
        )
    grad_mixed = grad_mixed.reshape(all_rows, width)
    grad_proj = [
        (grad_mixed * values).astype(bf16),
        grad_c.astype(bf16),
        (grad_mixed * gate_b).astype(bf16),
    ]
    grad_normed_in = relabel(
        against_rows(grad_proj[0], full_in[0])
        + against_rows(grad_proj[1], full_in[1])
        + against_rows(grad_proj[2], full_in[2])
    )
    back_in, gain_in_grad = norm_back(resid, scale_in, gain_in, grad_normed_in)
    grad_inputs = (grad_middle + back_in).reshape(micros, rows, width)

    def to_rows(term, extra=None):
        parts = [term[j * owned : (j + 1) * owned].astype(bf16) for j in range(peers)]
        if extra is not None:
            parts = [
                jnp.concatenate([part, more.astype(bf16)], axis=0)
                for part, more in zip(parts, extra)
            ]
        return sum_over_groups(scatter_relative(parts))

    grad_w_out = to_rows(over_tokens(gated, grad_branch))
    small_grads = relabel(jnp.stack([gain_in_grad, gain_mid_grad] + tap_terms))
    small_parts = []
    for j in range(peers):
        part = small_grads[:, j * owned : (j + 1) * owned].reshape(-1)
        small_parts.append(
            jnp.pad(part, (0, small_rows * width - part.shape[0])).reshape(small_rows, width)
        )
    grad_in_b = to_rows(over_tokens(normed_in, grad_proj[0]))
    grad_in_c = to_rows(over_tokens(normed_in, grad_proj[1]))
    grad_in_v = to_rows(over_tokens(normed_in, grad_proj[2]), small_parts)
    grad_w_in = jnp.concatenate([grad_in_b, grad_in_c, grad_in_v[:owned]], axis=1)
    small_owned = grad_in_v[owned:].reshape(-1)[:count].reshape(reach + 3, owned)
    return (
        block_out,
        grad_inputs,
        small_owned[0],
        grad_w_in,
        small_owned[2:],
        grad_w_out,
        small_owned[1],
        grad_w_gate,
        grad_w_up,
        grad_w_down,
    )


def solution(mesh):
    return jax.shard_map(
        per_device,
        mesh=mesh,
        in_specs=(
            P("dp", "fsdp", None),
            P("fsdp"),
            P("fsdp", None),
            P(None, "fsdp"),
            P("fsdp", None),
            P("fsdp"),
            P("fsdp", None),
            P("fsdp", None),
            P("fsdp", None),
            P("dp", "fsdp", None),
        ),
        out_specs=(
            P("dp", "fsdp", None),
            P("dp", "fsdp", None),
            P("fsdp"),
            P("fsdp", None),
            P(None, "fsdp"),
            P("fsdp", None),
            P("fsdp"),
            P("fsdp", None),
            P("fsdp", None),
            P("fsdp", None),
        ),
        check_vma=False,
    )
```

```python
import jax
import jax.numpy as jnp
from jax import lax
from jax.sharding import PartitionSpec as P

epsilon = 1e-05
bf16 = jnp.bfloat16
f32 = jnp.float32


def along(shard, axis, pairs):
    return lax.ppermute(shard, axis, pairs)


def after(value, *others):
    return lax.optimization_barrier((value,) + others)[0]


def flip(shard, bits):
    peers = lax.axis_size("fsdp")
    return along(shard, "fsdp", [(i, i ^ bits) for i in range(peers)])


def flip_by_core(shard, even_bits, odd_bits):
    peers = lax.axis_size("fsdp")
    return along(
        shard, "fsdp", [(i, i ^ (odd_bits if i & 1 else even_bits)) for i in range(peers)]
    )


def is_cube():
    return lax.axis_size("fsdp") == 8


def on_odd_core():
    return (lax.axis_index("fsdp") & 1) == 1


def gather_parts(shard):
    if not is_cube():
        return [lax.all_gather(shard, "fsdp", axis=0)], ()
    from_x = flip(shard, 2)
    from_y = flip(shard, 4)
    across = flip_by_core(jnp.where(on_odd_core(), from_y, from_x), 4, 2)
    mine = jnp.stack([shard, from_x, from_y])
    theirs = flip(mine, 1)
    last = flip(across, 1)
    return [theirs, last[None], mine, across[None]], (from_x, from_y)


def gather(shard):
    parts, first = gather_parts(shard)
    return jnp.concatenate(parts, axis=0), first


def places():
    return [1, 3, 5, 7, 0, 2, 4, 6] if is_cube() else list(range(lax.axis_size("fsdp")))


def scatter(theirs, mine):
    peers = lax.axis_size("fsdp")
    theirs = theirs.astype(bf16)
    if not is_cube():
        whole = jnp.concatenate([theirs, mine.astype(bf16)], axis=0)
        whole = whole.reshape(peers, whole.shape[0] // peers, -1)
        return lax.psum_scatter(whole, "fsdp", scatter_dimension=0).astype(f32), ()
    size = mine.shape[0] // 4
    near = flip(theirs, 1)
    mine = [mine[k * size : (k + 1) * size].astype(f32) for k in range(4)]
    mine = [mine[k] + near[k * size : (k + 1) * size] for k in range(4)]
    odd = on_odd_core()
    across = flip_by_core(mine[3].astype(bf16), 2, 4)
    zero = jnp.zeros((), f32)
    to_x = (mine[1] + jnp.where(odd, across.astype(f32), zero)).astype(bf16)
    to_y = (mine[2] + jnp.where(odd, zero, across.astype(f32))).astype(bf16)
    return mine[0] + flip(to_x, 2) + flip(to_y, 4), (near, across)


def exchange_parts(blocks):
    if not is_cube():
        return [lax.all_to_all(blocks, "fsdp", 0, 0)]
    chip, odd = lax.axis_index("fsdp") >> 1, on_odd_core()
    pairs = blocks.reshape((4, 2) + blocks.shape[1:])
    to_even, to_odd = pairs[:, 0], pairs[:, 1]
    kept = jnp.where(odd, to_odd, to_even)
    came = flip(jnp.where(odd, to_even, to_odd), 1)
    both = jnp.stack([jnp.where(odd, came, kept), jnp.where(odd, kept, came)], axis=1)
    return [both] + [
        flip(lax.dynamic_index_in_dim(both, chip ^ k, 0, keepdims=False), 2 * k)
        for k in (1, 2, 3)
    ]


def exchanged(parts):
    if not is_cube():
        return parts[0]
    chip, result = lax.axis_index("fsdp") >> 1, parts[0]
    for k in (1, 2, 3):
        result = lax.dynamic_update_index_in_dim(result, parts[k], chip ^ k, 0)
    return result.reshape((8,) + result.shape[2:])


def relabel(columns, back=False):
    peers = lax.axis_size("fsdp")
    if not is_cube():
        return columns
    size = columns.shape[-1] // peers
    me = lax.axis_index("fsdp")
    blocks = [columns[..., k * size : (k + 1) * size] for k in range(peers)]
    if back:
        blocks = [blocks[places().index(j)] for j in range(peers)]
    for bit in (1, 2, 4):
        swap = (me & bit) != 0
        blocks = [jnp.where(swap, blocks[k ^ bit], blocks[k]) for k in range(peers)]
    if not back:
        blocks = [blocks[j] for j in places()]
    return jnp.concatenate(blocks, axis=-1)


def in_line():
    return lax.axis_size("dp") == 4


def inward(term):
    if not in_line():
        return lax.psum(term, "dp")
    return along(term, "dp", [(0, 1), (3, 2)])


def between(pair):
    return along(pair, "dp", [(1, 2), (2, 1)]) if in_line() else pair


def outward(total):
    return along(total, "dp", [(1, 0), (2, 3)]) if in_line() else total


def add_pair(one, other):
    return (one.astype(f32) + other.astype(f32)).astype(bf16) if in_line() else other


def settle(total, came):
    if not in_line():
        return total
    inner = (lax.axis_index("dp") == 1) | (lax.axis_index("dp") == 2)
    return jnp.where(inner, total, came)


def together(*values):
    return lax.optimization_barrier(values)


def from_behind(shard, axis, by):
    peers = lax.axis_size(axis)
    pairs = [(i, i + by) for i in range(peers) if 0 <= i + by < peers]
    return lax.ppermute(shard, axis, pairs)


def inverse_rms(values):
    return lax.rsqrt(jnp.mean(values * values, axis=-1, keepdims=True) + epsilon)


def norm_back(values, scale, gain, incoming):
    normed = values * scale
    gain_grad = jnp.sum(incoming * normed, axis=0)
    weighted = incoming * gain
    projection = jnp.mean(weighted * normed, axis=-1, keepdims=True)
    return (scale * (weighted - normed * projection), gain_grad)


def times(left, right):
    return jnp.dot(left, right, preferred_element_type=f32)


def over_tokens(left, right):
    return lax.dot_general(left, right, (((0,), (0,)), ((), ())), preferred_element_type=f32)


def against_rows(left, right):
    return lax.dot_general(left, right, (((1,), (1,)), ((), ())), preferred_element_type=f32)


def per_device(inputs, norm_in, w_in, taps, w_out, norm_mid, w_gate, w_up, w_down, cotangent):
    micros, rows, width = inputs.shape
    peers = lax.axis_size("fsdp")
    reach = taps.shape[0] - 1
    owned = w_in.shape[0]
    hidden = w_down.shape[0]
    all_rows = micros * rows

    gate_up = jnp.concatenate(
        [jnp.transpose(w.reshape(owned, peers, hidden), (1, 0, 2)) for w in (w_gate, w_up)],
        axis=1,
    )
    gate_up = exchange_parts(gate_up)
    whole, first = gather(w_in)
    full_in = whole.reshape(width, 3 * width)
    smalls = jnp.concatenate([norm_in[None], norm_mid[None], taps], axis=0)
    smalls = jnp.pad(smalls, ((0, 8 - (reach + 3)), (0, 0)))
    smalls = jnp.transpose(gather(smalls)[0][:, : reach + 3], (1, 0, 2))
    smalls = relabel(smalls.reshape(reach + 3, width), back=True).astype(f32)
    gain_in, gain_mid, tap_values = smalls[0], smalls[1], smalls[2:]
    out_parts, first = gather_parts(after(w_out, *first))
    full_out = jnp.concatenate(out_parts, axis=0).reshape(width, width)
    grad_out = cotangent.reshape(all_rows, width)
    grad_out_parts = gather_parts(after(grad_out, *gate_up[1:], *out_parts[-1:]))[0]
    early = gate_up[1:]
    gate_up = exchanged(gate_up)
    own_gate = gate_up[:, :owned].reshape(width, hidden)
    own_up = gate_up[:, owned:].reshape(width, hidden)

    resid = inputs.reshape(all_rows, width).astype(f32)
    scale_in = inverse_rms(resid)
    normed_in = relabel((resid * scale_in * gain_in).astype(bf16))
    normed_in = after(normed_in, *early)
    projected = times(normed_in, full_in)
    gate_b = projected[:, :width]
    gate_c = projected[:, width : 2 * width]
    values = projected[:, 2 * width :]
    mixed = (gate_b * values).astype(bf16).reshape(micros, rows, width)
    earlier = from_behind(mixed[:, rows - reach :], "fsdp", 1)
    extended = jnp.concatenate([earlier, mixed], axis=1).astype(f32)
    convolved = jnp.zeros((micros, rows, width), f32)
    for offset in range(reach + 1):
        convolved = convolved + tap_values[offset] * extended[:, offset : offset + rows]
    convolved = convolved.reshape(all_rows, width)
    gated = relabel((gate_c * convolved).astype(bf16))
    middle = resid + times(gated, full_out)
    scale_mid = inverse_rms(middle)
    normed_mid = (middle * scale_mid * gain_mid).astype(bf16)

    normed_mid = after(normed_mid, *grad_out_parts)
    grad_out_all = jnp.concatenate(grad_out_parts, axis=0).reshape(peers * all_rows, width)
    normed_all = gather(normed_mid)[0].reshape(peers * all_rows, width)
    gate_pre = times(normed_all, own_gate)
    up_pre = times(normed_all, own_up)
    sigmoid_gate = jax.nn.sigmoid(gate_pre)
    activ = (gate_pre * sigmoid_gate * up_pre).astype(bf16)
    grad_activ = against_rows(grad_out_all, w_down)
    grad_gate = (
        grad_activ * up_pre * sigmoid_gate * (1.0 + gate_pre * (1.0 - sigmoid_gate))
    ).astype(bf16)
    grad_up = (grad_activ * gate_pre * sigmoid_gate).astype(bf16)
    half = peers * all_rows // 2

    def through_gates(part):
        return (
            against_rows(grad_gate[part], own_gate) + against_rows(grad_up[part], own_up)
        ).astype(bf16)

    theirs, ours = through_gates(slice(None, half)), through_gates(slice(half, None))
    grad_normed_mid, steps_mid = scatter(theirs, ours)

    gate_now, up_now = together(grad_gate, grad_up, theirs, ours)[:2]
    term_gate = over_tokens(normed_all, gate_now).astype(bf16)
    came_gate = inward(term_gate)
    up_now, activ_now = together(up_now, activ, term_gate)[:2]
    term_up = over_tokens(normed_all, up_now).astype(bf16)
    term_down = over_tokens(activ_now, grad_out_all).astype(bf16)
    half = peers * all_rows // 2
    final_theirs = times(activ_now[:half], w_down).astype(bf16)
    final_ours = times(activ_now[half:], w_down).astype(bf16)
    grad_normed_mid, came_gate, term_up = together(
        grad_normed_mid, came_gate, after(term_up, term_down, final_theirs, final_ours)
    )
    pair_gate = add_pair(term_gate, came_gate)
    far_gate = between(pair_gate)
    came_up = inward(term_up)

    back_mid, gain_mid_grad = norm_back(middle, scale_mid, gain_mid, grad_normed_mid)
    grad_middle = grad_out.astype(f32) + back_mid
    grad_branch = grad_middle.astype(bf16)
    grad_gated = relabel(against_rows(grad_branch, full_out), back=True)
    grad_c = grad_gated * convolved
    grad_conv = (grad_gated * gate_c).astype(bf16).reshape(micros, rows, width)
    later = from_behind(grad_conv[:, :reach], "fsdp", -1)
    ext_grad = jnp.concatenate([grad_conv, later], axis=1).astype(f32)
    grad_mixed = jnp.zeros((micros, rows, width), f32)
    tap_terms = []
    for offset in range(reach + 1):
        grad_mixed = (
            grad_mixed + tap_values[offset] * ext_grad[:, reach - offset : reach - offset + rows]
        )
        tap_terms.append(
            jnp.sum(extended[:, offset : offset + rows] * ext_grad[:, :rows], axis=(0, 1))
        )
    grad_mixed = grad_mixed.reshape(all_rows, width)
    grad_proj = [
        (grad_mixed * values).astype(bf16),
        grad_c.astype(bf16),
        (grad_mixed * gate_b).astype(bf16),
    ]

    grad_branch, far_gate, came_up, *grad_proj = together(
        grad_branch, far_gate, came_up, *grad_proj
    )
    half = width // 2
    normed_theirs, normed_ours = normed_in[:, :half], normed_in[:, half:]
    grad_b_v = jnp.concatenate([grad_proj[0], grad_proj[2]], axis=1)
    rows_out_c = scatter(
        *[
            jnp.concatenate([over_tokens(p, grad_branch), over_tokens(q, grad_proj[1])], axis=1)
            for p, q in ((gated[:, :half], normed_theirs), (gated[:, half:], normed_ours))
        ]
    )[0].astype(bf16)
    grad_normed_in = relabel(
        against_rows(jnp.concatenate(grad_proj, axis=1), full_in), back=True
    )
    back_in, gain_in_grad = norm_back(resid, scale_in, gain_in, grad_normed_in)
    grad_inputs = (grad_middle + back_in).reshape(micros, rows, width)
    smalls = relabel(jnp.stack([gain_in_grad, gain_mid_grad] + tap_terms))
    smalls = jnp.pad(jnp.transpose(smalls), ((0, 0), (0, 128 - (reach + 3))))
    rows_b_v = scatter(
        jnp.concatenate([over_tokens(normed_theirs, grad_b_v), smalls[:half]], axis=1),
        jnp.concatenate([over_tokens(normed_ours, grad_b_v), smalls[half:]], axis=1),
    )[0].astype(bf16)

    total_gate = add_pair(pair_gate, far_gate)
    out_gate = outward(total_gate)
    pair_up = add_pair(term_up, came_up)
    far_up = between(pair_up)
    came_down = inward(after(term_down, far_gate))

    rows_out_c, out_gate, far_up, came_down = together(rows_out_c, out_gate, far_up, came_down)
    total_up = add_pair(pair_up, far_up)
    out_up = outward(total_up)
    pair_down = add_pair(term_down, came_down)
    far_down = between(pair_down)
    came_out_c = inward(rows_out_c)
    mine_gate = exchange_parts(settle(total_gate, out_gate).reshape(peers, owned, hidden))
    final = scatter(after(final_theirs, rows_out_c), final_ours)[0]
    block_out = (middle + final).astype(bf16).reshape(micros, rows, width)

    rows_b_v, out_up, far_down, came_out_c, *mine_gate = together(
        rows_b_v, out_up, far_down, came_out_c, *mine_gate
    )
    total_down = add_pair(pair_down, far_down)
    out_down = outward(total_down)
    pair_out_c = add_pair(rows_out_c, came_out_c)
    far_out_c = between(pair_out_c)
    came_b_v = inward(rows_b_v)
    mine_up = exchange_parts(settle(total_up, out_up).reshape(peers, owned, hidden))

    out_down, far_out_c, came_b_v, *mine_up = together(out_down, far_out_c, came_b_v, *mine_up)
    total_out_c = add_pair(pair_out_c, far_out_c)
    out_out_c = outward(total_out_c)
    pair_b_v = add_pair(rows_b_v, came_b_v)
    total_b_v = add_pair(pair_b_v, between(pair_b_v))
    grad_w_down = settle(total_down, out_down).astype(f32)
    grad_w_gate, grad_w_up = [
        jnp.transpose(exchanged(parts), (1, 0, 2)).reshape(owned, peers * hidden).astype(f32)
        for parts in (mine_gate, mine_up)
    ]
    total_out_c = settle(total_out_c, out_out_c).astype(f32)
    total_b_v = settle(total_b_v, outward(total_b_v)).astype(f32)
    grad_w_out = total_out_c[:, :width]
    grad_w_in = jnp.concatenate(
        [total_b_v[:, :width], total_out_c[:, width:], total_b_v[:, width : 2 * width]], axis=1
    )
    smalls = jnp.transpose(total_b_v[:, 2 * width : 2 * width + reach + 3])
    return (
        block_out,
        grad_inputs,
        smalls[0],
        grad_w_in,
        smalls[2:],
        grad_w_out,
        smalls[1],
        grad_w_gate,
        grad_w_up,
        grad_w_down,
    )


def solution(mesh):
    return jax.shard_map(
        per_device,
        mesh=mesh,
        in_specs=(
            P("dp", "fsdp", None),
            P("fsdp"),
            P("fsdp", None),
            P(None, "fsdp"),
            P("fsdp", None),
            P("fsdp"),
            P("fsdp", None),
            P("fsdp", None),
            P("fsdp", None),
            P("dp", "fsdp", None),
        ),
        out_specs=(
            P("dp", "fsdp", None),
            P("dp", "fsdp", None),
            P("fsdp"),
            P("fsdp", None),
            P(None, "fsdp"),
            P("fsdp", None),
            P("fsdp"),
            P("fsdp", None),
            P("fsdp", None),
            P("fsdp", None),
        ),
        check_vma=False,
    )
```

```python
import jax
import jax.numpy as jnp
from jax import lax
from jax.experimental import pallas as pl
from jax.experimental.layout import Layout, with_layout_constraint
from jax.experimental.pallas import tpu as pltpu
from jax.sharding import PartitionSpec as P

epsilon = 1e-05
bf16 = jnp.bfloat16
f32 = jnp.float32


def along(shard, axis, pairs):
    return lax.ppermute(shard, axis, pairs)


def flip(shard, bits):
    peers = lax.axis_size("fsdp")
    return along(shard, "fsdp", [(i, i ^ bits) for i in range(peers)])


def flip_by_core(shard, even_bits, odd_bits):
    peers = lax.axis_size("fsdp")
    return along(
        shard, "fsdp", [(i, i ^ (odd_bits if i & 1 else even_bits)) for i in range(peers)]
    )


def is_cube():
    return lax.axis_size("fsdp") == 8


def on_odd_core():
    return (lax.axis_index("fsdp") & 1) == 1


def gather_sides(shard):
    if not is_cube():
        return (lax.all_gather(shard, "fsdp", axis=0),) * 2
    return flip(shard, 2), flip(shard, 4)


def gather_rest(shard, from_x, from_y):
    if not is_cube():
        return [from_x]
    across = flip_by_core(jnp.where(on_odd_core(), from_y, from_x), 4, 2)
    mine = jnp.stack([shard, from_x, from_y])
    return [flip(mine, 1), flip(across, 1)[None], mine, across[None]]


def gather(shard):
    return jnp.concatenate(gather_rest(shard, *gather_sides(shard)), axis=0)


def places():
    return [1, 3, 5, 7, 0, 2, 4, 6] if is_cube() else list(range(lax.axis_size("fsdp")))


def scatter_near(theirs, mine):
    if is_cube():
        return flip(theirs, 1)
    peers = lax.axis_size("fsdp")
    whole = jnp.concatenate([theirs, mine], axis=0)
    whole = whole.reshape(peers, whole.shape[0] // peers, -1)
    return lax.psum_scatter(whole, "fsdp", scatter_dimension=0)


def block_sum(mine, near, k):
    size = mine.shape[0] // 4
    rows = slice(k * size, (k + 1) * size)
    return mine[rows].astype(f32) + near[rows].astype(f32)


def scatter_across(mine, near):
    return flip_by_core(block_sum(mine, near, 3).astype(bf16), 2, 4) if is_cube() else near


def scatter_last(mine, near, across):
    if not is_cube():
        return near, near
    odd, zero = on_odd_core(), jnp.zeros((), f32)
    across = across.astype(f32)
    to_x = block_sum(mine, near, 1) + jnp.where(odd, across, zero)
    to_y = block_sum(mine, near, 2) + jnp.where(odd, zero, across)
    return flip(to_x.astype(bf16), 2), flip(to_y.astype(bf16), 4)


def scattered(mine, near, last):
    if not is_cube():
        return near.astype(f32)
    return block_sum(mine, near, 0) + last[0].astype(f32) + last[1].astype(f32)


def exchange_early(blocks):
    if not is_cube():
        return [lax.all_to_all(blocks, "fsdp", 0, 0)]
    chip, odd = lax.axis_index("fsdp") >> 1, on_odd_core()
    pairs = blocks.reshape((4, 2) + blocks.shape[1:])
    to_even, to_odd = pairs[:, 0], pairs[:, 1]
    kept = jnp.where(odd, to_odd, to_even)
    came = flip(jnp.where(odd, to_even, to_odd), 1)
    both = jnp.stack([jnp.where(odd, came, kept), jnp.where(odd, kept, came)], axis=1)
    return [both] + [
        flip(lax.dynamic_index_in_dim(both, chip ^ k, 0, keepdims=False), 2 * k)
        for k in (1, 2, 3)
    ]


def exchanged_early(parts):
    if not is_cube():
        return parts[0]
    chip, result = lax.axis_index("fsdp") >> 1, parts[0]
    for k in (1, 2, 3):
        result = lax.dynamic_update_index_in_dim(result, parts[k], chip ^ k, 0)
    return result.reshape((8,) + result.shape[2:])


def exchange_chips(blocks):
    if not is_cube():
        return [lax.all_to_all(blocks, "fsdp", 0, 0)]
    chip = lax.axis_index("fsdp") >> 1
    pairs = blocks.reshape((4, 2) + blocks.shape[1:])
    return [pairs] + [
        flip(lax.dynamic_index_in_dim(pairs, chip ^ k, 0, keepdims=False), 2 * k)
        for k in (1, 2, 3)
    ]


def exchange_cores(parts):
    if not is_cube():
        return parts[0]
    chip, odd = lax.axis_index("fsdp") >> 1, on_odd_core()
    came = parts[0]
    for k in (1, 2, 3):
        came = lax.dynamic_update_index_in_dim(came, parts[k], chip ^ k, 0)
    to_even, to_odd = came[:, 0], came[:, 1]
    kept = jnp.where(odd, to_odd, to_even)
    other = flip(jnp.where(odd, to_even, to_odd), 1)
    both = jnp.stack([jnp.where(odd, other, kept), jnp.where(odd, kept, other)], axis=1)
    return both.reshape((8,) + both.shape[2:])


def relabel(columns, back=False):
    peers = lax.axis_size("fsdp")
    if not is_cube():
        return columns
    size = columns.shape[-1] // peers
    me = lax.axis_index("fsdp")
    blocks = [columns[..., k * size : (k + 1) * size] for k in range(peers)]
    if back:
        blocks = [blocks[places().index(j)] for j in range(peers)]
    for bit in (1, 2, 4):
        swap = (me & bit) != 0
        blocks = [jnp.where(swap, blocks[k ^ bit], blocks[k]) for k in range(peers)]
    if not back:
        blocks = [blocks[j] for j in places()]
    return jnp.concatenate(blocks, axis=-1)


def in_line():
    return lax.axis_size("dp") == 4


def inward(term):
    if not in_line():
        return lax.psum(term, "dp")
    return along(term, "dp", [(0, 1), (3, 2)])


def between(pair):
    return along(pair, "dp", [(1, 2), (2, 1)]) if in_line() else pair


def outward(total):
    return along(total, "dp", [(1, 0), (2, 3)]) if in_line() else total


def inward_outward(term, total):
    if not in_line():
        return lax.psum(term, "dp"), total
    came = along(jnp.where(in_middle(), total, term), "dp", [(0, 1), (3, 2), (1, 0), (2, 3)])
    return jnp.where(in_middle(), came, jnp.zeros((), bf16)), came


def in_middle():
    return (lax.axis_index("dp") == 1) | (lax.axis_index("dp") == 2)


def add_pair(one, other):
    return (one.astype(f32) + other.astype(f32)).astype(bf16) if in_line() else other


def settle(total, came):
    if not in_line():
        return total
    return jnp.where(in_middle(), total, came)


def together(*values):
    return lax.optimization_barrier(values)


def from_behind(shard, axis, by):
    peers = lax.axis_size(axis)
    pairs = [(i, i + by) for i in range(peers) if 0 <= i + by < peers]
    return lax.ppermute(shard, axis, pairs)


def inverse_rms(values):
    return lax.rsqrt(jnp.mean(values * values, axis=-1, keepdims=True) + epsilon)


def norm_back(values, scale, gain, incoming):
    normed = values * scale
    gain_grad = jnp.sum(incoming * normed, axis=0)
    weighted = incoming * gain
    projection = jnp.mean(weighted * normed, axis=-1, keepdims=True)
    return (scale * (weighted - normed * projection), gain_grad)


def times(left, right):
    return jnp.dot(left, right, preferred_element_type=f32)


def over_tokens(left, right):
    return lax.dot_general(left, right, (((0,), (0,)), ((), ())), preferred_element_type=f32)


def against_rows(left, right):
    return lax.dot_general(left, right, (((1,), (1,)), ((), ())), preferred_element_type=f32)


def gated(gate_pre, up_pre, grad_activ):
    sigmoid_gate = jax.nn.sigmoid(gate_pre)
    silu_gate = gate_pre * sigmoid_gate
    activ = (silu_gate * up_pre).astype(bf16)
    grad_gate = (grad_activ * up_pre * (sigmoid_gate + silu_gate * (1.0 - sigmoid_gate))).astype(
        bf16
    )
    return activ, grad_gate, (grad_activ * silu_gate).astype(bf16)


def feed_forward_kernel(
    tokens_ref, grad_ref, gate_ref, up_ref, down_ref,
    activ_ref, grad_gate_ref, grad_up_ref, *out_refs,
):
    step, steps = pl.program_id(0), pl.num_programs(0)
    tokens, grad_out = tokens_ref[...], grad_ref[...]
    activ, grad_gate, grad_up = gated(
        against_rows(gate_ref[...], tokens),
        against_rows(up_ref[...], tokens),
        against_rows(down_ref[...], grad_out),
    )
    activ_ref[...], grad_gate_ref[...], grad_up_ref[...] = activ, grad_gate, grad_up
    back = over_tokens(grad_gate, gate_ref[...]) + over_tokens(grad_up, up_ref[...])
    back, final = back.astype(bf16), over_tokens(activ, down_ref[...]).astype(bf16)

    @pl.when(step < steps // 2)
    def _():
        out_refs[0][...] = back
        out_refs[2][...] = final

    @pl.when(step >= steps // 2)
    def _():
        out_refs[1][...] = back
        out_refs[3][...] = final


def feed_forward(tokens, grad_out, own_gate, own_up, own_down):
    count, width = tokens.shape
    hidden = own_gate.shape[0]
    half, tile = count // 2, 512
    if not is_cube() or half % tile or width % 128 or hidden % 16:
        activ, grad_gate, grad_up = gated(
            against_rows(own_gate, tokens),
            against_rows(own_up, tokens),
            against_rows(own_down, grad_out),
        )
        back = over_tokens(grad_gate, own_gate) + over_tokens(grad_up, own_up)
        back, final = back.astype(bf16), over_tokens(activ, own_down).astype(bf16)
        return activ, grad_gate, grad_up, back[:half], back[half:], final[:half], final[half:]
    steps = count // tile
    rows = pl.BlockSpec((tile, width), lambda i: (i, 0))
    whole = pl.BlockSpec((hidden, width), lambda i: (0, 0))
    columns = pl.BlockSpec((hidden, tile), lambda i: (0, i))
    first = pl.BlockSpec((tile, width), lambda i: (jnp.minimum(i, steps // 2 - 1), 0))
    second = pl.BlockSpec((tile, width), lambda i: (jnp.maximum(i - steps // 2, 0), 0))
    return pl.pallas_call(
        feed_forward_kernel,
        grid=(steps,),
        in_specs=[rows, rows, whole, whole, whole],
        out_specs=[columns] * 3 + [first, second] * 2,
        out_shape=[jax.ShapeDtypeStruct((hidden, count), bf16)] * 3
        + [jax.ShapeDtypeStruct((half, width), bf16)] * 4,
        compiler_params=pltpu.CompilerParams(vmem_limit_bytes=48 << 20),
        cost_estimate=pl.CostEstimate(
            flops=12 * count * width * hidden,
            bytes_accessed=2 * (4 * count * width + 3 * hidden * (width + count)),
            transcendentals=count * hidden,
        ),
    )(tokens, grad_out, own_gate, own_up, own_down)


def per_device(inputs, norm_in, w_in, taps, w_out, norm_mid, w_gate, w_up, w_down, cotangent):
    micros, rows_held, width = inputs.shape
    peers = lax.axis_size("fsdp")
    reach = taps.shape[0] - 1
    owned = w_in.shape[0]
    hidden = w_down.shape[0]
    all_rows = micros * rows_held

    gate_up = [jnp.transpose(w).reshape(peers, hidden, owned) for w in (w_gate, w_up)]
    groups = lax.axis_size("dp")
    if groups % 2 == 0:
        one_way = (lax.axis_index("dp") & 1) == 0
        gate_up = jnp.where(one_way, gate_up[0], gate_up[1])
    else:
        gate_up = jnp.concatenate(gate_up, axis=1)
    gate_up = exchange_early(gate_up)
    full_in = gather(w_in).reshape(width, 3 * width)
    smalls = jnp.concatenate([norm_in[None], norm_mid[None], taps], axis=0)
    smalls = jnp.pad(smalls, ((0, 8 - (reach + 3)), (0, 0)))
    smalls = jnp.transpose(gather(smalls)[:, : reach + 3], (1, 0, 2))
    smalls = relabel(smalls.reshape(reach + 3, width), back=True).astype(f32)
    gain_in, gain_mid, tap_values = smalls[0], smalls[1], smalls[2:]
    full_out = gather(w_out).reshape(width, width)
    grad_out = cotangent.reshape(all_rows, width)
    grad_out_all = gather(grad_out).reshape(peers * all_rows, width)
    gate_up = jnp.transpose(exchanged_early(gate_up), (1, 0, 2)).reshape(-1, width)
    if groups % 2 == 0:
        other = along(gate_up, "dp", [(i, i ^ 1) for i in range(groups)])
        own_gate = jnp.where(one_way, gate_up, other)
        own_up = jnp.where(one_way, other, gate_up)
    else:
        own_gate, own_up = gate_up[:hidden], gate_up[hidden:]

    resid = inputs.reshape(all_rows, width).astype(f32)
    scale_in = inverse_rms(resid)
    normed_in = relabel((resid * scale_in * gain_in).astype(bf16))
    projected = times(normed_in, full_in)
    gate_b = projected[:, :width]
    gate_c = projected[:, width : 2 * width]
    values = projected[:, 2 * width :]
    mixed = (gate_b * values).astype(bf16).reshape(micros, rows_held, width)
    earlier = from_behind(mixed[:, rows_held - reach :], "fsdp", 1)
    extended = jnp.concatenate([earlier, mixed], axis=1).astype(f32)
    convolved = jnp.zeros((micros, rows_held, width), f32)
    for offset in range(reach + 1):
        convolved = convolved + tap_values[offset] * extended[:, offset : offset + rows_held]
    convolved = convolved.reshape(all_rows, width)
    gated = relabel((gate_c * convolved).astype(bf16))
    middle = resid + times(gated, full_out)
    scale_mid = inverse_rms(middle)
    normed_mid = (middle * scale_mid * gain_mid).astype(bf16)

    normed_all = gather(normed_mid).reshape(peers * all_rows, width)
    activ, grad_gate, grad_up, theirs, ours, final_theirs, final_ours = feed_forward(
        normed_all, grad_out_all, own_gate, own_up, w_down
    )
    near = scatter_near(theirs, ours)

    term_gate = times(grad_gate, normed_all).astype(bf16)
    came_gate = inward(term_gate)
    near, grad_up, activ, term_gate = together(near, grad_up, activ, term_gate)
    across = scatter_across(ours, near)
    grad_normed_mid = scattered(ours, near, scatter_last(ours, near, across))
    term_up = times(grad_up, normed_all).astype(bf16)
    term_down = times(activ, grad_out_all).astype(bf16)
    grad_normed_mid, came_gate, term_up, term_down = together(
        grad_normed_mid, came_gate, term_up, term_down
    )
    came_up = inward(term_up)
    pair_gate = add_pair(term_gate, came_gate)
    far_gate = between(pair_gate)

    back_mid, gain_mid_grad = norm_back(middle, scale_mid, gain_mid, grad_normed_mid)
    grad_middle = grad_out.astype(f32) + back_mid
    grad_branch = grad_middle.astype(bf16)
    grad_gated = relabel(against_rows(grad_branch, full_out), back=True)
    grad_c = grad_gated * convolved
    grad_conv = (grad_gated * gate_c).astype(bf16).reshape(micros, rows_held, width)
    later = from_behind(grad_conv[:, :reach], "fsdp", -1)
    ext_grad = jnp.concatenate([grad_conv, later], axis=1).astype(f32)
    grad_mixed = jnp.zeros((micros, rows_held, width), f32)
    tap_terms = []
    for offset in range(reach + 1):
        grad_mixed = (
            grad_mixed + tap_values[offset] * ext_grad[:, reach - offset : reach - offset + rows_held]
        )
        tap_terms.append(
            jnp.sum(extended[:, offset : offset + rows_held] * ext_grad[:, :rows_held], axis=(0, 1))
        )
    grad_mixed = grad_mixed.reshape(all_rows, width)
    grad_proj = [
        (grad_mixed * values).astype(bf16),
        grad_c.astype(bf16),
        (grad_mixed * gate_b).astype(bf16),
    ]

    half = width // 2
    normed_theirs, normed_ours = normed_in[:, :half], normed_in[:, half:]
    grad_b_v = jnp.concatenate([grad_proj[0], grad_proj[2]], axis=1)
    terms_out_c = [
        jnp.concatenate(
            [over_tokens(p, grad_branch).astype(bf16), over_tokens(q, grad_proj[1]).astype(bf16)],
            axis=1,
        )
        for p, q in ((gated[:, :half], normed_theirs), (gated[:, half:], normed_ours))
    ]
    terms_b_v = [over_tokens(p, grad_b_v).astype(bf16) for p in (normed_theirs, normed_ours)]
    grad_normed_in = relabel(
        against_rows(jnp.concatenate(grad_proj, axis=1), full_in), back=True
    )
    back_in, gain_in_grad = norm_back(resid, scale_in, gain_in, grad_normed_in)
    grad_inputs = (grad_middle + back_in).reshape(micros, rows_held, width)
    smalls = relabel(jnp.stack([gain_in_grad, gain_mid_grad] + tap_terms))
    smalls = jnp.pad(jnp.transpose(smalls), ((0, 0), (0, 128 - (reach + 3)))).astype(bf16)
    terms_b_v = [
        jnp.concatenate([terms_b_v[0], smalls[:half]], axis=1),
        jnp.concatenate([terms_b_v[1], smalls[half:]], axis=1),
    ]
    near_out_c = scatter_near(*terms_out_c)
    across_out_c = scatter_across(terms_out_c[1], near_out_c)
    across_out_c, terms_b_v[0], far_gate, came_up, term_down = together(
        across_out_c, terms_b_v[0], far_gate, came_up, term_down
    )

    total_gate = add_pair(pair_gate, far_gate)
    both = inward_outward(term_down, total_gate)
    pair_up = add_pair(term_up, came_up)
    far_up = between(pair_up)
    last_out_c = scatter_last(terms_out_c[1], near_out_c, across_out_c)
    near_b_v = scatter_near(*terms_b_v)
    across_b_v = scatter_across(terms_b_v[1], near_b_v)

    came_down, out_gate, far_up, across_b_v, *last_out_c = together(
        *both, far_up, across_b_v, *last_out_c
    )
    rows_out_c = scattered(terms_out_c[1], near_out_c, last_out_c).astype(bf16)
    came_out_c = inward(rows_out_c)
    pair_down = add_pair(term_down, came_down)
    far_down = between(pair_down)
    total_up = add_pair(pair_up, far_up)
    out_up = outward(total_up)
    last_b_v = scatter_last(terms_b_v[1], near_b_v, across_b_v)

    came_out_c, out_up, far_down, final_theirs, *last_b_v = together(
        came_out_c, out_up, far_down, final_theirs, *last_b_v
    )
    rows_b_v = scattered(terms_b_v[1], near_b_v, last_b_v).astype(bf16)
    came_b_v = inward(rows_b_v)
    pair_out_c = add_pair(rows_out_c, came_out_c)
    far_out_c = between(pair_out_c)
    total_down = add_pair(pair_down, far_down)
    out_down = outward(total_down)
    mine = exchange_chips(
        jnp.concatenate(
            [
                jnp.transpose(settle(t, o).reshape(hidden, peers, owned), (1, 0, 2))
                for t, o in ((total_gate, out_gate), (total_up, out_up))
            ],
            axis=1,
        )
    )

    came_b_v, far_out_c, out_down, final_theirs, *mine = together(
        came_b_v, far_out_c, out_down, final_theirs, *mine
    )
    pair_b_v = add_pair(rows_b_v, came_b_v)
    far_b_v = between(pair_b_v)
    total_out_c = add_pair(pair_out_c, far_out_c)
    out_out_c = outward(total_out_c)
    near_final = scatter_near(final_theirs, final_ours)
    across_final = scatter_across(final_ours, near_final)
    grad_w_down = settle(total_down, out_down).astype(f32)
    mine = exchange_cores(mine)
    by_rows = Layout(major_to_minor=(0, 1))
    grad_w_gate, grad_w_up = [
        with_layout_constraint(
            jnp.transpose(part.reshape(peers * hidden, owned)).astype(f32), by_rows
        )
        for part in (mine[:, :hidden], mine[:, hidden:])
    ]

    far_b_v, out_out_c, across_final, grad_w_down, grad_w_gate, grad_w_up = together(
        far_b_v, out_out_c, across_final, grad_w_down, grad_w_gate, grad_w_up
    )
    total_b_v = add_pair(pair_b_v, far_b_v)
    out_b_v = outward(total_b_v)
    last_final = scatter_last(final_ours, near_final, across_final)
    final = scattered(final_ours, near_final, last_final)
    block_out = (middle + final).astype(bf16).reshape(micros, rows_held, width)
    out_b_v, block_out = together(out_b_v, block_out)
    total_out_c = settle(total_out_c, out_out_c).astype(f32)
    total_b_v = settle(total_b_v, out_b_v).astype(f32)
    grad_w_out = total_out_c[:, :width]
    grad_w_in = jnp.concatenate(
        [total_b_v[:, :width], total_out_c[:, width:], total_b_v[:, width : 2 * width]], axis=1
    )
    smalls = jnp.transpose(total_b_v[:, 2 * width : 2 * width + reach + 3])
    return (
        block_out,
        grad_inputs,
        smalls[0],
        grad_w_in,
        smalls[2:],
        grad_w_out,
        smalls[1],
        grad_w_gate,
        grad_w_up,
        grad_w_down,
    )


def solution(mesh):
    return jax.shard_map(
        per_device,
        mesh=mesh,
        in_specs=(
            P("dp", "fsdp", None),
            P("fsdp"),
            P("fsdp", None),
            P(None, "fsdp"),
            P("fsdp", None),
            P("fsdp"),
            P("fsdp", None),
            P("fsdp", None),
            P("fsdp", None),
            P("dp", "fsdp", None),
        ),
        out_specs=(
            P("dp", "fsdp", None),
            P("dp", "fsdp", None),
            P("fsdp"),
            P("fsdp", None),
            P(None, "fsdp"),
            P("fsdp", None),
            P("fsdp"),
            P("fsdp", None),
            P("fsdp", None),
            P("fsdp", None),
        ),
        check_vma=False,
    )
```

```python
import jax
import jax.numpy as jnp
from jax import lax
from jax.experimental import pallas as pl
from jax.experimental.layout import Layout, with_layout_constraint
from jax.experimental.pallas import tpu as pltpu
from jax.sharding import PartitionSpec as P

epsilon = 1e-05
bf16 = jnp.bfloat16
f32 = jnp.float32


def along(shard, axis, pairs):
    return lax.ppermute(shard, axis, pairs)


def flip(shard, bits):
    peers = lax.axis_size("fsdp")
    return along(shard, "fsdp", [(i, i ^ bits) for i in range(peers)])


def flip_by_core(shard, even_bits, odd_bits):
    peers = lax.axis_size("fsdp")
    return along(
        shard, "fsdp", [(i, i ^ (odd_bits if i & 1 else even_bits)) for i in range(peers)]
    )


def is_cube():
    return lax.axis_size("fsdp") == 8


def on_odd_core():
    return (lax.axis_index("fsdp") & 1) == 1


def gather_sides(shard):
    if not is_cube():
        return (lax.all_gather(shard, "fsdp", axis=0),) * 2
    return flip(shard, 2), flip(shard, 4)


def gather_rest(shard, from_x, from_y):
    if not is_cube():
        return [from_x]
    across = flip_by_core(jnp.where(on_odd_core(), from_y, from_x), 4, 2)
    mine = jnp.stack([shard, from_x, from_y])
    return [flip(mine, 1), flip(across, 1)[None], mine, across[None]]


def gather(shard):
    return jnp.concatenate(gather_rest(shard, *gather_sides(shard)), axis=0)


def places():
    return [1, 3, 5, 7, 0, 2, 4, 6] if is_cube() else list(range(lax.axis_size("fsdp")))


def scatter_near(theirs, mine):
    if is_cube():
        return flip(theirs, 1)
    peers = lax.axis_size("fsdp")
    whole = jnp.concatenate([theirs, mine], axis=0)
    whole = whole.reshape(peers, whole.shape[0] // peers, -1)
    return lax.psum_scatter(whole, "fsdp", scatter_dimension=0)


def block_sum(mine, near, k):
    size = mine.shape[0] // 4
    rows = slice(k * size, (k + 1) * size)
    return mine[rows].astype(f32) + near[rows].astype(f32)


def scatter_across(mine, near):
    return flip_by_core(block_sum(mine, near, 3).astype(bf16), 2, 4) if is_cube() else near


def scatter_last(mine, near, across):
    if not is_cube():
        return near, near
    odd, zero = on_odd_core(), jnp.zeros((), f32)
    across = across.astype(f32)
    to_x = block_sum(mine, near, 1) + jnp.where(odd, across, zero)
    to_y = block_sum(mine, near, 2) + jnp.where(odd, zero, across)
    return flip(to_x.astype(bf16), 2), flip(to_y.astype(bf16), 4)


def scattered(mine, near, last):
    if not is_cube():
        return near.astype(f32)
    return block_sum(mine, near, 0) + last[0].astype(f32) + last[1].astype(f32)


def exchange_early_cores(blocks):
    if not is_cube():
        return blocks
    odd = on_odd_core()
    pairs = blocks.reshape((4, 2) + blocks.shape[1:])
    to_even, to_odd = pairs[:, 0], pairs[:, 1]
    kept = jnp.where(odd, to_odd, to_even)
    came = flip(jnp.where(odd, to_even, to_odd), 1)
    return jnp.stack([jnp.where(odd, came, kept), jnp.where(odd, kept, came)], axis=1)


def exchange_early_chips(both):
    if not is_cube():
        return [lax.all_to_all(both, "fsdp", 0, 0)]
    chip = lax.axis_index("fsdp") >> 1
    return [both] + [
        flip(lax.dynamic_index_in_dim(both, chip ^ k, 0, keepdims=False), 2 * k)
        for k in (1, 2, 3)
    ]


def exchanged_early(parts):
    if not is_cube():
        return parts[0]
    chip, result = lax.axis_index("fsdp") >> 1, parts[0]
    for k in (1, 2, 3):
        result = lax.dynamic_update_index_in_dim(result, parts[k], chip ^ k, 0)
    return result.reshape((8,) + result.shape[2:])


def exchange_chips(blocks):
    if not is_cube():
        return [lax.all_to_all(blocks, "fsdp", 0, 0)]
    chip = lax.axis_index("fsdp") >> 1
    pairs = blocks.reshape((4, 2) + blocks.shape[1:])
    return [pairs] + [
        flip(lax.dynamic_index_in_dim(pairs, chip ^ k, 0, keepdims=False), 2 * k)
        for k in (1, 2, 3)
    ]


def exchange_cores(parts):
    if not is_cube():
        return parts[0]
    chip, odd = lax.axis_index("fsdp") >> 1, on_odd_core()
    came = parts[0]
    for k in (1, 2, 3):
        came = lax.dynamic_update_index_in_dim(came, parts[k], chip ^ k, 0)
    to_even, to_odd = came[:, 0], came[:, 1]
    kept = jnp.where(odd, to_odd, to_even)
    other = flip(jnp.where(odd, to_even, to_odd), 1)
    both = jnp.stack([jnp.where(odd, other, kept), jnp.where(odd, kept, other)], axis=1)
    return both.reshape((8,) + both.shape[2:])


def relabel(columns, back=False):
    peers = lax.axis_size("fsdp")
    if not is_cube():
        return columns
    size = columns.shape[-1] // peers
    me = lax.axis_index("fsdp")
    blocks = [columns[..., k * size : (k + 1) * size] for k in range(peers)]
    if back:
        blocks = [blocks[places().index(j)] for j in range(peers)]
    for bit in (1, 2, 4):
        swap = (me & bit) != 0
        blocks = [jnp.where(swap, blocks[k ^ bit], blocks[k]) for k in range(peers)]
    if not back:
        blocks = [blocks[j] for j in places()]
    return jnp.concatenate(blocks, axis=-1)


def in_line():
    return lax.axis_size("dp") == 4


def inward(term):
    if not in_line():
        return lax.psum(term, "dp")
    return along(term, "dp", [(0, 1), (3, 2)])


def between(pair):
    return along(pair, "dp", [(1, 2), (2, 1)]) if in_line() else pair


def outward(total):
    return along(total, "dp", [(1, 0), (2, 3)]) if in_line() else total


def inward_outward(term, total):
    if not in_line():
        return lax.psum(term, "dp"), total
    came = along(jnp.where(in_middle(), total, term), "dp", [(0, 1), (3, 2), (1, 0), (2, 3)])
    return jnp.where(in_middle(), came, jnp.zeros((), bf16)), came


def in_middle():
    return (lax.axis_index("dp") == 1) | (lax.axis_index("dp") == 2)


def add_pair(one, other):
    return (one.astype(f32) + other.astype(f32)).astype(bf16) if in_line() else other


def settle(total, came):
    if not in_line():
        return total
    return jnp.where(in_middle(), total, came)


def together(*values):
    return lax.optimization_barrier(values)


def from_behind(shard, axis, by):
    peers = lax.axis_size(axis)
    pairs = [(i, i + by) for i in range(peers) if 0 <= i + by < peers]
    return lax.ppermute(shard, axis, pairs)


def inverse_rms(values):
    return lax.rsqrt(jnp.mean(values * values, axis=-1, keepdims=True) + epsilon)


def norm_back(values, scale, gain, incoming):
    normed = values * scale
    gain_grad = jnp.sum(incoming * normed, axis=0)
    weighted = incoming * gain
    projection = jnp.mean(weighted * normed, axis=-1, keepdims=True)
    return (scale * (weighted - normed * projection), gain_grad)


def times(left, right):
    return jnp.dot(left, right, preferred_element_type=f32)


def over_tokens(left, right):
    return lax.dot_general(left, right, (((0,), (0,)), ((), ())), preferred_element_type=f32)


def against_rows(left, right):
    return lax.dot_general(left, right, (((1,), (1,)), ((), ())), preferred_element_type=f32)


def gated(gate_pre, up_pre, grad_activ):
    sigmoid_gate = jax.nn.sigmoid(gate_pre)
    silu_gate = gate_pre * sigmoid_gate
    activ = (silu_gate * up_pre).astype(bf16)
    grad_gate = (grad_activ * up_pre * (sigmoid_gate + silu_gate * (1.0 - sigmoid_gate))).astype(
        bf16
    )
    return activ, grad_gate, (grad_activ * silu_gate).astype(bf16)


def feed_forward_kernel(
    tokens_ref, grad_ref, gate_ref, up_ref, down_ref,
    activ_ref, grad_gate_ref, grad_up_ref, *out_refs,
):
    step, steps = pl.program_id(0), pl.num_programs(0)
    tokens, grad_out = tokens_ref[...], grad_ref[...]
    activ, grad_gate, grad_up = gated(
        against_rows(gate_ref[...], tokens),
        against_rows(up_ref[...], tokens),
        against_rows(down_ref[...], grad_out),
    )
    activ_ref[...], grad_gate_ref[...], grad_up_ref[...] = activ, grad_gate, grad_up
    back = over_tokens(grad_gate, gate_ref[...]) + over_tokens(grad_up, up_ref[...])
    back, final = back.astype(bf16), over_tokens(activ, down_ref[...]).astype(bf16)

    @pl.when(step < steps // 2)
    def _():
        out_refs[0][...] = back
        out_refs[2][...] = final

    @pl.when(step >= steps // 2)
    def _():
        out_refs[1][...] = back
        out_refs[3][...] = final


def feed_forward(tokens, grad_out, own_gate, own_up, own_down):
    count, width = tokens.shape
    hidden = own_gate.shape[0]
    half, tile = count // 2, 512
    if not is_cube() or half % tile or width % 128 or hidden % 16:
        activ, grad_gate, grad_up = gated(
            against_rows(own_gate, tokens),
            against_rows(own_up, tokens),
            against_rows(own_down, grad_out),
        )
        back = over_tokens(grad_gate, own_gate) + over_tokens(grad_up, own_up)
        back, final = back.astype(bf16), over_tokens(activ, own_down).astype(bf16)
        return activ, grad_gate, grad_up, back[:half], back[half:], final[:half], final[half:]
    steps = count // tile
    rows = pl.BlockSpec((tile, width), lambda i: (i, 0))
    whole = pl.BlockSpec((hidden, width), lambda i: (0, 0))
    columns = pl.BlockSpec((hidden, tile), lambda i: (0, i))
    first = pl.BlockSpec((tile, width), lambda i: (jnp.minimum(i, steps // 2 - 1), 0))
    second = pl.BlockSpec((tile, width), lambda i: (jnp.maximum(i - steps // 2, 0), 0))
    return pl.pallas_call(
        feed_forward_kernel,
        grid=(steps,),
        in_specs=[rows, rows, whole, whole, whole],
        out_specs=[columns] * 3 + [first, second] * 2,
        out_shape=[jax.ShapeDtypeStruct((hidden, count), bf16)] * 3
        + [jax.ShapeDtypeStruct((half, width), bf16)] * 4,
        compiler_params=pltpu.CompilerParams(vmem_limit_bytes=48 << 20),
        cost_estimate=pl.CostEstimate(
            flops=12 * count * width * hidden,
            bytes_accessed=2 * (4 * count * width + 3 * hidden * (width + count)),
            transcendentals=count * hidden,
        ),
    )(tokens, grad_out, own_gate, own_up, own_down)


def per_device(inputs, norm_in, w_in, taps, w_out, norm_mid, w_gate, w_up, w_down, cotangent):
    micros, rows_held, width = inputs.shape
    peers = lax.axis_size("fsdp")
    reach = taps.shape[0] - 1
    owned = w_in.shape[0]
    hidden = w_down.shape[0]
    all_rows = micros * rows_held

    gate_up = [jnp.transpose(w).reshape(peers, hidden, owned) for w in (w_gate, w_up)]
    groups = lax.axis_size("dp")
    if groups % 2 == 0:
        one_way = (lax.axis_index("dp") & 1) == 0
        gate_up = jnp.where(one_way, gate_up[0], gate_up[1])
    else:
        gate_up = jnp.concatenate(gate_up, axis=1)
    grad_out = cotangent.reshape(all_rows, width)
    gate_up = exchange_early_cores(gate_up)
    in_x, in_y, w_out = together(*gather_sides(w_in), w_out)
    in_parts = gather_rest(w_in, in_x, in_y)
    out_x, out_y, in_parts[-1], gate_up = together(
        *gather_sides(w_out), in_parts[-1], gate_up
    )
    out_parts = gather_rest(w_out, out_x, out_y)
    grad_out_now, *gate_up = together(grad_out, *exchange_early_chips(gate_up))
    full_in = jnp.concatenate(in_parts, axis=0).reshape(width, 3 * width)
    smalls = jnp.concatenate([norm_in[None], norm_mid[None], taps], axis=0)
    smalls = jnp.pad(smalls, ((0, 8 - (reach + 3)), (0, 0)))
    smalls = jnp.transpose(gather(smalls)[:, : reach + 3], (1, 0, 2))
    smalls = relabel(smalls.reshape(reach + 3, width), back=True).astype(f32)
    gain_in, gain_mid, tap_values = smalls[0], smalls[1], smalls[2:]
    full_out = jnp.concatenate(out_parts, axis=0).reshape(width, width)
    grad_out_x, grad_out_y = gather_sides(grad_out_now)
    gate_up = jnp.transpose(exchanged_early(gate_up), (1, 0, 2)).reshape(-1, width)
    if groups % 2 == 0:
        other = along(gate_up, "dp", [(i, i ^ 1) for i in range(groups)])
        own_gate = jnp.where(one_way, gate_up, other)
        own_up = jnp.where(one_way, other, gate_up)
    else:
        own_gate, own_up = gate_up[:hidden], gate_up[hidden:]

    resid = inputs.reshape(all_rows, width).astype(f32)
    scale_in = inverse_rms(resid)
    normed_in = relabel((resid * scale_in * gain_in).astype(bf16))
    projected = times(normed_in, full_in)
    gate_b = projected[:, :width]
    gate_c = projected[:, width : 2 * width]
    values = projected[:, 2 * width :]
    mixed = (gate_b * values).astype(bf16).reshape(micros, rows_held, width)
    earlier = from_behind(mixed[:, rows_held - reach :], "fsdp", 1)
    extended = jnp.concatenate([earlier, mixed], axis=1).astype(f32)
    convolved = jnp.zeros((micros, rows_held, width), f32)
    for offset in range(reach + 1):
        convolved = convolved + tap_values[offset] * extended[:, offset : offset + rows_held]
    convolved = convolved.reshape(all_rows, width)
    gated = relabel((gate_c * convolved).astype(bf16))
    middle = resid + times(gated, full_out)
    scale_mid = inverse_rms(middle)
    normed_mid = (middle * scale_mid * gain_mid).astype(bf16)

    normed_mid, grad_out_x, grad_out_y = together(normed_mid, grad_out_x, grad_out_y)
    normed_all = gather(normed_mid).reshape(peers * all_rows, width)
    grad_out_all = jnp.concatenate(gather_rest(grad_out_now, grad_out_x, grad_out_y), axis=0)
    grad_out_all = grad_out_all.reshape(peers * all_rows, width)
    activ, grad_gate, grad_up, theirs, ours, final_theirs, final_ours = feed_forward(
        normed_all, grad_out_all, own_gate, own_up, w_down
    )
    near = scatter_near(theirs, ours)

    term_gate = times(grad_gate, normed_all).astype(bf16)
    came_gate = inward(term_gate)
    near, grad_up, activ, term_gate = together(near, grad_up, activ, term_gate)
    across = scatter_across(ours, near)
    grad_normed_mid = scattered(ours, near, scatter_last(ours, near, across))
    term_up = times(grad_up, normed_all).astype(bf16)
    term_down = times(activ, grad_out_all).astype(bf16)
    grad_normed_mid, came_gate, term_up, term_down = together(
        grad_normed_mid, came_gate, term_up, term_down
    )
    came_up = inward(term_up)
    pair_gate = add_pair(term_gate, came_gate)
    far_gate = between(pair_gate)

    back_mid, gain_mid_grad = norm_back(middle, scale_mid, gain_mid, grad_normed_mid)
    grad_middle = grad_out.astype(f32) + back_mid
    grad_branch = grad_middle.astype(bf16)
    grad_gated = relabel(against_rows(grad_branch, full_out), back=True)
    grad_c = grad_gated * convolved
    grad_conv = (grad_gated * gate_c).astype(bf16).reshape(micros, rows_held, width)
    later = from_behind(grad_conv[:, :reach], "fsdp", -1)
    ext_grad = jnp.concatenate([grad_conv, later], axis=1).astype(f32)
    grad_mixed = jnp.zeros((micros, rows_held, width), f32)
    tap_terms = []
    for offset in range(reach + 1):
        grad_mixed = (
            grad_mixed + tap_values[offset] * ext_grad[:, reach - offset : reach - offset + rows_held]
        )
        tap_terms.append(
            jnp.sum(extended[:, offset : offset + rows_held] * ext_grad[:, :rows_held], axis=(0, 1))
        )
    grad_mixed = grad_mixed.reshape(all_rows, width)
    grad_proj = [
        (grad_mixed * values).astype(bf16),
        grad_c.astype(bf16),
        (grad_mixed * gate_b).astype(bf16),
    ]

    half = width // 2
    normed_theirs, normed_ours = normed_in[:, :half], normed_in[:, half:]
    terms_out_c = [
        jnp.concatenate(
            [over_tokens(p, grad_branch).astype(bf16), over_tokens(q, grad_proj[1]).astype(bf16)],
            axis=1,
        )
        for p, q in ((gated[:, :half], normed_theirs), (gated[:, half:], normed_ours))
    ]
    near_out_c = scatter_near(*terms_out_c)
    near_out_c, grad_proj[0], grad_proj[2] = together(near_out_c, grad_proj[0], grad_proj[2])
    across_out_c = scatter_across(terms_out_c[1], near_out_c)
    grad_b_v = jnp.concatenate([grad_proj[0], grad_proj[2]], axis=1)
    terms_b_v = [over_tokens(p, grad_b_v).astype(bf16) for p in (normed_theirs, normed_ours)]
    grad_normed_in = relabel(
        against_rows(jnp.concatenate(grad_proj, axis=1), full_in), back=True
    )
    back_in, gain_in_grad = norm_back(resid, scale_in, gain_in, grad_normed_in)
    grad_inputs = (grad_middle + back_in).reshape(micros, rows_held, width)
    smalls = relabel(jnp.stack([gain_in_grad, gain_mid_grad] + tap_terms))
    smalls = jnp.pad(jnp.transpose(smalls), ((0, 0), (0, 128 - (reach + 3)))).astype(bf16)
    terms_b_v = [
        jnp.concatenate([terms_b_v[0], smalls[:half]], axis=1),
        jnp.concatenate([terms_b_v[1], smalls[half:]], axis=1),
    ]
    near_final = scatter_near(final_theirs, final_ours)
    across_out_c, *terms_b_v, far_gate, came_up, term_down, near_final = together(
        across_out_c, *terms_b_v, far_gate, came_up, term_down, near_final
    )

    total_gate = add_pair(pair_gate, far_gate)
    both = inward_outward(term_down, total_gate)
    pair_up = add_pair(term_up, came_up)
    far_up = between(pair_up)
    last_out_c = scatter_last(terms_out_c[1], near_out_c, across_out_c)
    near_b_v = scatter_near(*terms_b_v)
    across_b_v = scatter_across(terms_b_v[1], near_b_v)

    came_down, out_gate, far_up, across_b_v, *last_out_c = together(
        *both, far_up, across_b_v, *last_out_c
    )
    rows_out_c = scattered(terms_out_c[1], near_out_c, last_out_c).astype(bf16)
    came_out_c = inward(rows_out_c)
    pair_down = add_pair(term_down, came_down)
    far_down = between(pair_down)
    total_up = add_pair(pair_up, far_up)
    out_up = outward(total_up)
    last_b_v = scatter_last(terms_b_v[1], near_b_v, across_b_v)
    across_final = scatter_across(final_ours, near_final)

    came_out_c, out_up, far_down, across_final, *last_b_v = together(
        came_out_c, out_up, far_down, across_final, *last_b_v
    )
    rows_b_v = scattered(terms_b_v[1], near_b_v, last_b_v).astype(bf16)
    came_b_v = inward(rows_b_v)
    pair_out_c = add_pair(rows_out_c, came_out_c)
    far_out_c = between(pair_out_c)
    total_down = add_pair(pair_down, far_down)
    out_down = outward(total_down)
    mine = exchange_chips(
        jnp.concatenate(
            [
                jnp.transpose(settle(t, o).reshape(hidden, peers, owned), (1, 0, 2))
                for t, o in ((total_gate, out_gate), (total_up, out_up))
            ],
            axis=1,
        )
    )

    came_b_v, far_out_c, out_down, across_final, *mine = together(
        came_b_v, far_out_c, out_down, across_final, *mine
    )
    pair_b_v = add_pair(rows_b_v, came_b_v)
    far_b_v = between(pair_b_v)
    total_out_c = add_pair(pair_out_c, far_out_c)
    out_out_c = outward(total_out_c)
    last_final = scatter_last(final_ours, near_final, across_final)
    grad_w_down = settle(total_down, out_down).astype(f32)
    mine = exchange_cores(mine)
    by_rows = Layout(major_to_minor=(0, 1))
    grad_w_gate, grad_w_up = [
        with_layout_constraint(
            jnp.transpose(part.reshape(peers * hidden, owned)).astype(f32), by_rows
        )
        for part in (mine[:, :hidden], mine[:, hidden:])
    ]

    far_b_v, out_out_c, last_x, last_y, grad_w_down, grad_w_gate, grad_w_up = together(
        far_b_v, out_out_c, *last_final, grad_w_down, grad_w_gate, grad_w_up
    )
    total_b_v = add_pair(pair_b_v, far_b_v)
    out_b_v = outward(total_b_v)
    final = scattered(final_ours, near_final, (last_x, last_y))
    block_out = (middle + final).astype(bf16).reshape(micros, rows_held, width)
    out_b_v, block_out = together(out_b_v, block_out)
    total_out_c = settle(total_out_c, out_out_c).astype(f32)
    total_b_v = settle(total_b_v, out_b_v).astype(f32)
    grad_w_out = total_out_c[:, :width]
    grad_w_in = jnp.concatenate(
        [total_b_v[:, :width], total_out_c[:, width:], total_b_v[:, width : 2 * width]], axis=1
    )
    smalls = jnp.transpose(total_b_v[:, 2 * width : 2 * width + reach + 3])
    return (
        block_out,
        grad_inputs,
        smalls[0],
        grad_w_in,
        smalls[2:],
        grad_w_out,
        smalls[1],
        grad_w_gate,
        grad_w_up,
        grad_w_down,
    )


def solution(mesh):
    return jax.shard_map(
        per_device,
        mesh=mesh,
        in_specs=(
            P("dp", "fsdp", None),
            P("fsdp"),
            P("fsdp", None),
            P(None, "fsdp"),
            P("fsdp", None),
            P("fsdp"),
            P("fsdp", None),
            P("fsdp", None),
            P("fsdp", None),
            P("dp", "fsdp", None),
        ),
        out_specs=(
            P("dp", "fsdp", None),
            P("dp", "fsdp", None),
            P("fsdp"),
            P("fsdp", None),
            P(None, "fsdp"),
            P("fsdp", None),
            P("fsdp"),
            P("fsdp", None),
            P("fsdp", None),
            P("fsdp", None),
        ),
        check_vma=False,
    )
```

```python
import jax
import jax.numpy as jnp
from jax import lax
from jax.experimental import pallas as pl
from jax.experimental.layout import Layout, with_layout_constraint
from jax.experimental.pallas import tpu as pltpu
from jax.sharding import PartitionSpec as P

epsilon = 1e-05
bf16 = jnp.bfloat16
f32 = jnp.float32


def along(shard, axis, pairs):
    return lax.ppermute(shard, axis, pairs)


def flip(shard, bits):
    peers = lax.axis_size("fsdp")
    return along(shard, "fsdp", [(i, i ^ bits) for i in range(peers)])


def flip_by_core(shard, even_bits, odd_bits):
    peers = lax.axis_size("fsdp")
    return along(
        shard, "fsdp", [(i, i ^ (odd_bits if i & 1 else even_bits)) for i in range(peers)]
    )


def is_cube():
    return lax.axis_size("fsdp") == 8


def on_odd_core():
    return (lax.axis_index("fsdp") & 1) == 1


def gather_sides(shard):
    if not is_cube():
        return (lax.all_gather(shard, "fsdp", axis=0),) * 2
    return flip(shard, 2), flip(shard, 4)


def gather_rest(shard, from_x, from_y):
    if not is_cube():
        return [from_x]
    across = flip_by_core(jnp.where(on_odd_core(), from_y, from_x), 4, 2)
    mine = jnp.stack([shard, from_x, from_y])
    return [flip(mine, 1), flip(across, 1)[None], mine, across[None]]


def gather(shard):
    return jnp.concatenate(gather_rest(shard, *gather_sides(shard)), axis=0)


def places():
    return [1, 3, 5, 7, 0, 2, 4, 6] if is_cube() else list(range(lax.axis_size("fsdp")))


def scatter_near(theirs, mine):
    if is_cube():
        return flip(theirs, 1)
    peers = lax.axis_size("fsdp")
    whole = jnp.concatenate([theirs, mine], axis=0)
    whole = whole.reshape(peers, whole.shape[0] // peers, -1)
    return lax.psum_scatter(whole, "fsdp", scatter_dimension=0)


def block_sum(mine, near, k):
    size = mine.shape[0] // 4
    rows = slice(k * size, (k + 1) * size)
    return mine[rows].astype(f32) + near[rows].astype(f32)


def scatter_across(mine, near):
    return flip_by_core(block_sum(mine, near, 3).astype(bf16), 2, 4) if is_cube() else near


def scatter_last(mine, near, across):
    if not is_cube():
        return near, near
    odd, zero = on_odd_core(), jnp.zeros((), f32)
    across = across.astype(f32)
    to_x = block_sum(mine, near, 1) + jnp.where(odd, across, zero)
    to_y = block_sum(mine, near, 2) + jnp.where(odd, zero, across)
    return flip(to_x.astype(bf16), 2), flip(to_y.astype(bf16), 4)


def scattered(mine, near, last):
    if not is_cube():
        return near.astype(f32)
    return block_sum(mine, near, 0) + last[0].astype(f32) + last[1].astype(f32)


def exchange_early_cores(blocks):
    if not is_cube():
        return blocks
    odd = on_odd_core()
    pairs = blocks.reshape((4, 2) + blocks.shape[1:])
    to_even, to_odd = pairs[:, 0], pairs[:, 1]
    kept = jnp.where(odd, to_odd, to_even)
    came = flip(jnp.where(odd, to_even, to_odd), 1)
    return jnp.stack([jnp.where(odd, came, kept), jnp.where(odd, kept, came)], axis=1)


def exchange_early_chips(both):
    if not is_cube():
        return [lax.all_to_all(both, "fsdp", 0, 0)]
    chip = lax.axis_index("fsdp") >> 1
    return [both] + [
        flip(lax.dynamic_index_in_dim(both, chip ^ k, 0, keepdims=False), 2 * k)
        for k in (1, 2, 3)
    ]


def exchanged_early(parts):
    if not is_cube():
        return parts[0]
    chip, result = lax.axis_index("fsdp") >> 1, parts[0]
    for k in (1, 2, 3):
        result = lax.dynamic_update_index_in_dim(result, parts[k], chip ^ k, 0)
    return result.reshape((8,) + result.shape[2:])


def exchange_chips(blocks):
    if not is_cube():
        return [lax.all_to_all(blocks, "fsdp", 0, 0)]
    chip = lax.axis_index("fsdp") >> 1
    pairs = blocks.reshape((4, 2) + blocks.shape[1:])
    return [pairs] + [
        flip(lax.dynamic_index_in_dim(pairs, chip ^ k, 0, keepdims=False), 2 * k)
        for k in (1, 2, 3)
    ]


def exchange_cores(parts):
    if not is_cube():
        return parts[0]
    chip, odd = lax.axis_index("fsdp") >> 1, on_odd_core()
    came = parts[0]
    for k in (1, 2, 3):
        came = lax.dynamic_update_index_in_dim(came, parts[k], chip ^ k, 0)
    to_even, to_odd = came[:, 0], came[:, 1]
    kept = jnp.where(odd, to_odd, to_even)
    other = flip(jnp.where(odd, to_even, to_odd), 1)
    both = jnp.stack([jnp.where(odd, other, kept), jnp.where(odd, kept, other)], axis=1)
    return both.reshape((8,) + both.shape[2:])


def relabel(columns, back=False):
    peers = lax.axis_size("fsdp")
    if not is_cube():
        return columns
    size = columns.shape[-1] // peers
    me = lax.axis_index("fsdp")
    blocks = [columns[..., k * size : (k + 1) * size] for k in range(peers)]
    if back:
        blocks = [blocks[places().index(j)] for j in range(peers)]
    for bit in (1, 2, 4):
        swap = (me & bit) != 0
        blocks = [jnp.where(swap, blocks[k ^ bit], blocks[k]) for k in range(peers)]
    if not back:
        blocks = [blocks[j] for j in places()]
    return jnp.concatenate(blocks, axis=-1)


def in_line():
    return lax.axis_size("dp") == 4


def inward(term):
    if not in_line():
        return lax.psum(term, "dp")
    return along(term, "dp", [(0, 1), (3, 2)])


def between(pair):
    return along(pair, "dp", [(1, 2), (2, 1)]) if in_line() else pair


def outward(total):
    return along(total, "dp", [(1, 0), (2, 3)]) if in_line() else total


def inward_outward(term, total):
    if not in_line():
        return lax.psum(term, "dp"), total
    came = along(jnp.where(in_middle(), total, term), "dp", [(0, 1), (3, 2), (1, 0), (2, 3)])
    return jnp.where(in_middle(), came, jnp.zeros((), bf16)), came


def in_middle():
    return (lax.axis_index("dp") == 1) | (lax.axis_index("dp") == 2)


def add_pair(one, other):
    return (one.astype(f32) + other.astype(f32)).astype(bf16) if in_line() else other


def settle(total, came):
    if not in_line():
        return total
    return jnp.where(in_middle(), total, came)


def together(*values):
    return lax.optimization_barrier(values)


def from_behind(shard, axis, by):
    peers = lax.axis_size(axis)
    pairs = [(i, i + by) for i in range(peers) if 0 <= i + by < peers]
    return lax.ppermute(shard, axis, pairs)


def inverse_rms(values):
    return lax.rsqrt(jnp.mean(values * values, axis=-1, keepdims=True) + epsilon)


def norm_back(values, scale, gain, incoming):
    normed = values * scale
    gain_grad = jnp.sum(incoming * normed, axis=0)
    weighted = incoming * gain
    projection = jnp.mean(weighted * normed, axis=-1, keepdims=True)
    return (scale * (weighted - normed * projection), gain_grad)


def times(left, right):
    return jnp.dot(left, right, preferred_element_type=f32)


def over_tokens(left, right):
    return lax.dot_general(left, right, (((0,), (0,)), ((), ())), preferred_element_type=f32)


def against_rows(left, right):
    return lax.dot_general(left, right, (((1,), (1,)), ((), ())), preferred_element_type=f32)


def gated(gate_pre, up_pre, grad_activ):
    sigmoid_gate = jax.nn.sigmoid(gate_pre)
    silu_gate = gate_pre * sigmoid_gate
    activ = (silu_gate * up_pre).astype(bf16)
    grad_gate = (grad_activ * up_pre * (sigmoid_gate + silu_gate * (1.0 - sigmoid_gate))).astype(
        bf16
    )
    return activ, grad_gate, (grad_activ * silu_gate).astype(bf16)


def feed_forward_kernel(
    tokens_ref, grad_ref, gate_ref, up_ref, down_ref,
    activ_ref, grad_gate_ref, grad_up_ref, *out_refs,
):
    step, steps = pl.program_id(0), pl.num_programs(0)
    tokens, grad_out = tokens_ref[...], grad_ref[...]
    activ, grad_gate, grad_up = gated(
        against_rows(gate_ref[...], tokens),
        against_rows(up_ref[...], tokens),
        against_rows(down_ref[...], grad_out),
    )
    activ_ref[...], grad_gate_ref[...], grad_up_ref[...] = activ, grad_gate, grad_up
    back = over_tokens(grad_gate, gate_ref[...]) + over_tokens(grad_up, up_ref[...])
    back, final = back.astype(bf16), over_tokens(activ, down_ref[...]).astype(bf16)

    @pl.when(step < steps // 2)
    def _():
        out_refs[0][...] = back
        out_refs[2][...] = final

    @pl.when(step >= steps // 2)
    def _():
        out_refs[1][...] = back
        out_refs[3][...] = final


def feed_forward(tokens, grad_out, own_gate, own_up, own_down):
    count, width = tokens.shape
    hidden = own_gate.shape[0]
    half, tile = count // 2, 512
    if not is_cube() or half % tile or width % 128 or hidden % 16:
        activ, grad_gate, grad_up = gated(
            against_rows(own_gate, tokens),
            against_rows(own_up, tokens),
            against_rows(own_down, grad_out),
        )
        back = over_tokens(grad_gate, own_gate) + over_tokens(grad_up, own_up)
        back, final = back.astype(bf16), over_tokens(activ, own_down).astype(bf16)
        return activ, grad_gate, grad_up, back[:half], back[half:], final[:half], final[half:]
    steps = count // tile
    rows = pl.BlockSpec((tile, width), lambda i: (i, 0))
    whole = pl.BlockSpec((hidden, width), lambda i: (0, 0))
    columns = pl.BlockSpec((hidden, tile), lambda i: (0, i))
    first = pl.BlockSpec((tile, width), lambda i: (jnp.minimum(i, steps // 2 - 1), 0))
    second = pl.BlockSpec((tile, width), lambda i: (jnp.maximum(i - steps // 2, 0), 0))
    return pl.pallas_call(
        feed_forward_kernel,
        grid=(steps,),
        in_specs=[rows, rows, whole, whole, whole],
        out_specs=[columns] * 3 + [first, second] * 2,
        out_shape=[jax.ShapeDtypeStruct((hidden, count), bf16)] * 3
        + [jax.ShapeDtypeStruct((half, width), bf16)] * 4,
        compiler_params=pltpu.CompilerParams(vmem_limit_bytes=48 << 20),
        cost_estimate=pl.CostEstimate(
            flops=12 * count * width * hidden,
            bytes_accessed=2 * (4 * count * width + 3 * hidden * (width + count)),
            transcendentals=count * hidden,
        ),
    )(tokens, grad_out, own_gate, own_up, own_down)


def per_device(inputs, norm_in, w_in, taps, w_out, norm_mid, w_gate, w_up, w_down, cotangent):
    micros, rows_held, width = inputs.shape
    peers = lax.axis_size("fsdp")
    reach = taps.shape[0] - 1
    owned = w_in.shape[0]
    hidden = w_down.shape[0]
    all_rows = micros * rows_held

    gate_up = [jnp.transpose(w).reshape(peers, hidden, owned) for w in (w_gate, w_up)]
    groups = lax.axis_size("dp")
    if groups % 2 == 0:
        one_way = (lax.axis_index("dp") & 1) == 0
        gate_up = jnp.where(one_way, gate_up[0], gate_up[1])
    else:
        gate_up = jnp.concatenate(gate_up, axis=1)
    grad_out = cotangent.reshape(all_rows, width)
    gate_up = exchange_early_cores(gate_up)
    in_x, in_y, w_out = together(*gather_sides(w_in), w_out)
    in_parts = gather_rest(w_in, in_x, in_y)
    out_x, out_y, in_parts[-1], gate_up = together(
        *gather_sides(w_out), in_parts[-1], gate_up
    )
    out_parts = gather_rest(w_out, out_x, out_y)
    grad_out_now, *gate_up = together(grad_out, *exchange_early_chips(gate_up))
    full_in = jnp.concatenate(in_parts, axis=0).reshape(width, 3 * width)
    smalls = jnp.concatenate([norm_in[None], norm_mid[None], taps], axis=0)
    smalls = jnp.pad(smalls, ((0, 8 - (reach + 3)), (0, 0)))
    smalls = jnp.transpose(gather(smalls)[:, : reach + 3], (1, 0, 2))
    smalls = relabel(smalls.reshape(reach + 3, width), back=True).astype(f32)
    gain_in, gain_mid, tap_values = smalls[0], smalls[1], smalls[2:]
    full_out = jnp.concatenate(out_parts, axis=0).reshape(width, width)
    grad_out_x, grad_out_y = gather_sides(grad_out_now)
    gate_up = jnp.transpose(exchanged_early(gate_up), (1, 0, 2)).reshape(-1, width)
    if groups % 2 == 0:
        other = along(gate_up, "dp", [(i, i ^ 1) for i in range(groups)])
        own_gate = jnp.where(one_way, gate_up, other)
        own_up = jnp.where(one_way, other, gate_up)
    else:
        own_gate, own_up = gate_up[:hidden], gate_up[hidden:]

    resid = inputs.reshape(all_rows, width).astype(f32)
    scale_in = inverse_rms(resid)
    normed_in = relabel((resid * scale_in * gain_in).astype(bf16))
    projected = times(normed_in, full_in)
    gate_b = projected[:, :width]
    gate_c = projected[:, width : 2 * width]
    values = projected[:, 2 * width :]
    mixed = (gate_b * values).astype(bf16).reshape(micros, rows_held, width)
    earlier = from_behind(mixed[:, rows_held - reach :], "fsdp", 1)
    extended = jnp.concatenate([earlier, mixed], axis=1).astype(f32)
    convolved = jnp.zeros((micros, rows_held, width), f32)
    for offset in range(reach + 1):
        convolved = convolved + tap_values[offset] * extended[:, offset : offset + rows_held]
    convolved = convolved.reshape(all_rows, width)
    gated = relabel((gate_c * convolved).astype(bf16))
    middle = resid + times(gated, full_out)
    scale_mid = inverse_rms(middle)
    normed_mid = (middle * scale_mid * gain_mid).astype(bf16)

    normed_mid, grad_out_x, grad_out_y = together(normed_mid, grad_out_x, grad_out_y)
    normed_all = gather(normed_mid).reshape(peers * all_rows, width)
    grad_out_all = jnp.concatenate(gather_rest(grad_out_now, grad_out_x, grad_out_y), axis=0)
    grad_out_all = grad_out_all.reshape(peers * all_rows, width)
    activ, grad_gate, grad_up, theirs, ours, final_theirs, final_ours = feed_forward(
        normed_all, grad_out_all, own_gate, own_up, w_down
    )
    near = scatter_near(theirs, ours)

    term_gate = times(grad_gate, normed_all).astype(bf16)
    came_gate = inward(term_gate)
    near, grad_up, activ, term_gate = together(near, grad_up, activ, term_gate)
    across = scatter_across(ours, near)
    grad_normed_mid = scattered(ours, near, scatter_last(ours, near, across))
    term_up = times(grad_up, normed_all).astype(bf16)
    term_down = times(activ, grad_out_all).astype(bf16)
    grad_normed_mid, term_up, term_down = together(grad_normed_mid, term_up, term_down)
    came_up = inward(term_up)
    pair_gate = add_pair(term_gate, came_gate)
    far_gate = between(pair_gate)

    back_mid, gain_mid_grad = norm_back(middle, scale_mid, gain_mid, grad_normed_mid)
    grad_middle = grad_out.astype(f32) + back_mid
    grad_branch = grad_middle.astype(bf16)
    grad_gated = relabel(against_rows(grad_branch, full_out), back=True)
    grad_c = grad_gated * convolved
    grad_conv = (grad_gated * gate_c).astype(bf16).reshape(micros, rows_held, width)
    later = from_behind(grad_conv[:, :reach], "fsdp", -1)
    ext_grad = jnp.concatenate([grad_conv, later], axis=1).astype(f32)
    grad_mixed = jnp.zeros((micros, rows_held, width), f32)
    tap_terms = []
    for offset in range(reach + 1):
        grad_mixed = (
            grad_mixed + tap_values[offset] * ext_grad[:, reach - offset : reach - offset + rows_held]
        )
        tap_terms.append(
            jnp.sum(extended[:, offset : offset + rows_held] * ext_grad[:, :rows_held], axis=(0, 1))
        )
    grad_mixed = grad_mixed.reshape(all_rows, width)
    grad_proj = [
        (grad_mixed * values).astype(bf16),
        grad_c.astype(bf16),
        (grad_mixed * gate_b).astype(bf16),
    ]

    half = width // 2
    normed_theirs, normed_ours = normed_in[:, :half], normed_in[:, half:]
    terms_out_c = [
        jnp.concatenate(
            [over_tokens(p, grad_branch).astype(bf16), over_tokens(q, grad_proj[1]).astype(bf16)],
            axis=1,
        )
        for p, q in ((gated[:, :half], normed_theirs), (gated[:, half:], normed_ours))
    ]
    near_out_c = scatter_near(*terms_out_c)
    near_out_c, grad_proj[0], grad_proj[2] = together(near_out_c, grad_proj[0], grad_proj[2])
    across_out_c = scatter_across(terms_out_c[1], near_out_c)
    grad_b_v = jnp.concatenate([grad_proj[0], grad_proj[2]], axis=1)
    terms_b_v = [over_tokens(p, grad_b_v).astype(bf16) for p in (normed_theirs, normed_ours)]
    grad_normed_in = relabel(
        against_rows(jnp.concatenate(grad_proj, axis=1), full_in), back=True
    )
    back_in, gain_in_grad = norm_back(resid, scale_in, gain_in, grad_normed_in)
    grad_inputs = (grad_middle + back_in).reshape(micros, rows_held, width)
    smalls = relabel(jnp.stack([gain_in_grad, gain_mid_grad] + tap_terms))
    smalls = jnp.pad(jnp.transpose(smalls), ((0, 0), (0, 128 - (reach + 3)))).astype(bf16)
    terms_b_v = [
        jnp.concatenate([terms_b_v[0], smalls[:half]], axis=1),
        jnp.concatenate([terms_b_v[1], smalls[half:]], axis=1),
    ]
    near_final = scatter_near(final_theirs, final_ours)
    across_out_c, *terms_b_v, far_gate, came_up, term_down, near_final = together(
        across_out_c, *terms_b_v, far_gate, came_up, term_down, near_final
    )

    total_gate = add_pair(pair_gate, far_gate)
    both = inward_outward(term_down, total_gate)
    pair_up = add_pair(term_up, came_up)
    far_up = between(pair_up)
    last_out_c = scatter_last(terms_out_c[1], near_out_c, across_out_c)
    near_b_v = scatter_near(*terms_b_v)
    across_b_v = scatter_across(terms_b_v[1], near_b_v)

    came_down, out_gate, far_up, across_b_v, *last_out_c = together(
        *both, far_up, across_b_v, *last_out_c
    )
    rows_out_c = scattered(terms_out_c[1], near_out_c, last_out_c).astype(bf16)
    came_out_c = inward(rows_out_c)
    pair_down = add_pair(term_down, came_down)
    far_down = between(pair_down)
    total_up = add_pair(pair_up, far_up)
    out_up = outward(total_up)
    last_b_v = scatter_last(terms_b_v[1], near_b_v, across_b_v)
    across_final = scatter_across(final_ours, near_final)

    came_out_c, out_up, far_down, across_final, *last_b_v = together(
        came_out_c, out_up, far_down, across_final, *last_b_v
    )
    rows_b_v = scattered(terms_b_v[1], near_b_v, last_b_v).astype(bf16)
    came_b_v = inward(rows_b_v)
    pair_out_c = add_pair(rows_out_c, came_out_c)
    far_out_c = between(pair_out_c)
    total_down = add_pair(pair_down, far_down)
    out_down = outward(total_down)
    mine = exchange_chips(
        jnp.concatenate(
            [
                jnp.transpose(settle(t, o).reshape(hidden, peers, owned), (1, 0, 2))
                for t, o in ((total_gate, out_gate), (total_up, out_up))
            ],
            axis=1,
        )
    )

    came_b_v, far_out_c, out_down, across_final, *mine = together(
        came_b_v, far_out_c, out_down, across_final, *mine
    )
    pair_b_v = add_pair(rows_b_v, came_b_v)
    far_b_v = between(pair_b_v)
    total_out_c = add_pair(pair_out_c, far_out_c)
    out_out_c = outward(total_out_c)
    last_final = scatter_last(final_ours, near_final, across_final)
    grad_w_down = settle(total_down, out_down).astype(f32)
    mine = exchange_cores(mine)
    by_rows = Layout(major_to_minor=(0, 1))
    grad_w_gate, grad_w_up = [
        with_layout_constraint(
            jnp.transpose(part.reshape(peers * hidden, owned)).astype(f32), by_rows
        )
        for part in (mine[:, :hidden], mine[:, hidden:])
    ]

    far_b_v, out_out_c, last_x, last_y, grad_w_down, grad_w_gate, grad_w_up = together(
        far_b_v, out_out_c, *last_final, grad_w_down, grad_w_gate, grad_w_up
    )
    total_b_v = add_pair(pair_b_v, far_b_v)
    out_b_v = outward(total_b_v)
    final = scattered(final_ours, near_final, (last_x, last_y))
    block_out = (middle + final).astype(bf16).reshape(micros, rows_held, width)
    out_b_v, block_out = together(out_b_v, block_out)
    total_out_c = settle(total_out_c, out_out_c).astype(f32)
    total_b_v = settle(total_b_v, out_b_v).astype(f32)
    grad_w_out = total_out_c[:, :width]
    grad_w_in = jnp.concatenate(
        [total_b_v[:, :width], total_out_c[:, width:], total_b_v[:, width : 2 * width]], axis=1
    )
    smalls = jnp.transpose(total_b_v[:, 2 * width : 2 * width + reach + 3])
    return (
        block_out,
        grad_inputs,
        smalls[0],
        grad_w_in,
        smalls[2:],
        grad_w_out,
        smalls[1],
        grad_w_gate,
        grad_w_up,
        grad_w_down,
    )


def solution(mesh):
    return jax.shard_map(
        per_device,
        mesh=mesh,
        in_specs=(
            P("dp", "fsdp", None),
            P("fsdp"),
            P("fsdp", None),
            P(None, "fsdp"),
            P("fsdp", None),
            P("fsdp"),
            P("fsdp", None),
            P("fsdp", None),
            P("fsdp", None),
            P("dp", "fsdp", None),
        ),
        out_specs=(
            P("dp", "fsdp", None),
            P("dp", "fsdp", None),
            P("fsdp"),
            P("fsdp", None),
            P(None, "fsdp"),
            P("fsdp", None),
            P("fsdp"),
            P("fsdp", None),
            P("fsdp", None),
            P("fsdp", None),
        ),
        check_vma=False,
    )
```

```python
import jax
import jax.numpy as jnp
from jax import lax
from jax.experimental import pallas as pl
from jax.experimental.layout import Layout, with_layout_constraint
from jax.experimental.pallas import tpu as pltpu
from jax.sharding import PartitionSpec as P

epsilon = 1e-05
bf16 = jnp.bfloat16
f32 = jnp.float32


def along(shard, axis, pairs):
    return lax.ppermute(shard, axis, pairs)


def flip(shard, bits):
    peers = lax.axis_size("fsdp")
    return along(shard, "fsdp", [(i, i ^ bits) for i in range(peers)])


def flip_by_core(shard, even_bits, odd_bits):
    peers = lax.axis_size("fsdp")
    return along(
        shard, "fsdp", [(i, i ^ (odd_bits if i & 1 else even_bits)) for i in range(peers)]
    )


def is_cube():
    return lax.axis_size("fsdp") == 8


def on_odd_core():
    return (lax.axis_index("fsdp") & 1) == 1


def gather_sides(shard):
    if not is_cube():
        return (lax.all_gather(shard, "fsdp", axis=0),) * 2
    return flip(shard, 2), flip(shard, 4)


def gather_rest(shard, from_x, from_y):
    if not is_cube():
        return [from_x]
    across = flip_by_core(jnp.where(on_odd_core(), from_y, from_x), 4, 2)
    mine = jnp.stack([shard, from_x, from_y])
    return [flip(mine, 1), flip(across, 1)[None], mine, across[None]]


def gather(shard):
    return jnp.concatenate(gather_rest(shard, *gather_sides(shard)), axis=0)


def places():
    return [1, 3, 5, 7, 0, 2, 4, 6] if is_cube() else list(range(lax.axis_size("fsdp")))


def scatter_near(theirs, mine):
    if is_cube():
        return flip(theirs, 1)
    peers = lax.axis_size("fsdp")
    whole = jnp.concatenate([theirs, mine], axis=0)
    whole = whole.reshape(peers, whole.shape[0] // peers, -1)
    return lax.psum_scatter(whole, "fsdp", scatter_dimension=0)


def block_sum(mine, near, k):
    size = mine.shape[0] // 4
    rows = slice(k * size, (k + 1) * size)
    return mine[rows].astype(f32) + near[rows].astype(f32)


def scatter_across(mine, near):
    return flip_by_core(block_sum(mine, near, 3).astype(bf16), 2, 4) if is_cube() else near


def scatter_last(mine, near, across):
    if not is_cube():
        return near, near
    odd, zero = on_odd_core(), jnp.zeros((), f32)
    across = across.astype(f32)
    to_x = block_sum(mine, near, 1) + jnp.where(odd, across, zero)
    to_y = block_sum(mine, near, 2) + jnp.where(odd, zero, across)
    return flip(to_x.astype(bf16), 2), flip(to_y.astype(bf16), 4)


def scattered(mine, near, last):
    if not is_cube():
        return near.astype(f32)
    return block_sum(mine, near, 0) + last[0].astype(f32) + last[1].astype(f32)


def exchange_early_cores(blocks):
    if not is_cube():
        return blocks
    odd = on_odd_core()
    pairs = blocks.reshape((4, 2) + blocks.shape[1:])
    to_even, to_odd = pairs[:, 0], pairs[:, 1]
    kept = jnp.where(odd, to_odd, to_even)
    came = flip(jnp.where(odd, to_even, to_odd), 1)
    return jnp.stack([jnp.where(odd, came, kept), jnp.where(odd, kept, came)], axis=1)


def exchange_early_chips(both):
    if not is_cube():
        return [lax.all_to_all(both, "fsdp", 0, 0)]
    chip = lax.axis_index("fsdp") >> 1
    return [both] + [
        flip(lax.dynamic_index_in_dim(both, chip ^ k, 0, keepdims=False), 2 * k)
        for k in (1, 2, 3)
    ]


def exchanged_early(parts):
    if not is_cube():
        return parts[0]
    chip, result = lax.axis_index("fsdp") >> 1, parts[0]
    for k in (1, 2, 3):
        result = lax.dynamic_update_index_in_dim(result, parts[k], chip ^ k, 0)
    return result.reshape((8,) + result.shape[2:])


def exchange_chips(blocks):
    if not is_cube():
        return [lax.all_to_all(blocks, "fsdp", 0, 0)]
    chip = lax.axis_index("fsdp") >> 1
    pairs = blocks.reshape((4, 2) + blocks.shape[1:])
    return [pairs] + [
        flip(lax.dynamic_index_in_dim(pairs, chip ^ k, 0, keepdims=False), 2 * k)
        for k in (1, 2, 3)
    ]


def exchange_cores(parts):
    if not is_cube():
        return parts[0]
    chip, odd = lax.axis_index("fsdp") >> 1, on_odd_core()
    came = parts[0]
    for k in (1, 2, 3):
        came = lax.dynamic_update_index_in_dim(came, parts[k], chip ^ k, 0)
    to_even, to_odd = came[:, 0], came[:, 1]
    kept = jnp.where(odd, to_odd, to_even)
    other = flip(jnp.where(odd, to_even, to_odd), 1)
    both = jnp.stack([jnp.where(odd, other, kept), jnp.where(odd, kept, other)], axis=1)
    return both.reshape((8,) + both.shape[2:])


def relabel(columns, back=False):
    peers = lax.axis_size("fsdp")
    if not is_cube():
        return columns
    size = columns.shape[-1] // peers
    me = lax.axis_index("fsdp")
    blocks = [columns[..., k * size : (k + 1) * size] for k in range(peers)]
    if back:
        blocks = [blocks[places().index(j)] for j in range(peers)]
    for bit in (1, 2, 4):
        swap = (me & bit) != 0
        blocks = [jnp.where(swap, blocks[k ^ bit], blocks[k]) for k in range(peers)]
    if not back:
        blocks = [blocks[j] for j in places()]
    return jnp.concatenate(blocks, axis=-1)


def in_line():
    return lax.axis_size("dp") == 4


def inward(term):
    if not in_line():
        return lax.psum(term, "dp")
    return along(term, "dp", [(0, 1), (3, 2)])


def between(pair):
    return along(pair, "dp", [(1, 2), (2, 1)]) if in_line() else pair


def outward(total):
    return along(total, "dp", [(1, 0), (2, 3)]) if in_line() else total


def inward_outward(term, total):
    if not in_line():
        return lax.psum(term, "dp"), total
    came = along(jnp.where(in_middle(), total, term), "dp", [(0, 1), (3, 2), (1, 0), (2, 3)])
    return jnp.where(in_middle(), came, jnp.zeros((), bf16)), came


def in_middle():
    return (lax.axis_index("dp") == 1) | (lax.axis_index("dp") == 2)


def add_pair(one, other):
    return (one.astype(f32) + other.astype(f32)).astype(bf16) if in_line() else other


def settle(total, came):
    if not in_line():
        return total
    return jnp.where(in_middle(), total, came)


def together(*values):
    return lax.optimization_barrier(values)


def from_behind(shard, axis, by):
    peers = lax.axis_size(axis)
    pairs = [(i, i + by) for i in range(peers) if 0 <= i + by < peers]
    return lax.ppermute(shard, axis, pairs)


def inverse_rms(values):
    return lax.rsqrt(jnp.mean(values * values, axis=-1, keepdims=True) + epsilon)


def norm_back(values, scale, gain, incoming):
    normed = values * scale
    gain_grad = jnp.sum(incoming * normed, axis=0)
    weighted = incoming * gain
    projection = jnp.mean(weighted * normed, axis=-1, keepdims=True)
    return (scale * (weighted - normed * projection), gain_grad)


def times(left, right):
    return jnp.dot(left, right, preferred_element_type=f32)


def over_tokens(left, right):
    return lax.dot_general(left, right, (((0,), (0,)), ((), ())), preferred_element_type=f32)


def against_rows(left, right):
    return lax.dot_general(left, right, (((1,), (1,)), ((), ())), preferred_element_type=f32)


def gated(gate_pre, up_pre, grad_activ):
    sigmoid_gate = jax.nn.sigmoid(gate_pre)
    silu_gate = gate_pre * sigmoid_gate
    activ = (silu_gate * up_pre).astype(bf16)
    grad_gate = (grad_activ * up_pre * (sigmoid_gate + silu_gate * (1.0 - sigmoid_gate))).astype(
        bf16
    )
    return activ, grad_gate, (grad_activ * silu_gate).astype(bf16)


def feed_forward_kernel(
    tokens_ref, grad_ref, gate_ref, up_ref, down_ref,
    activ_ref, grad_gate_ref, grad_up_ref, *out_refs,
):
    step, steps = pl.program_id(0), pl.num_programs(0)
    tokens, grad_out = tokens_ref[...], grad_ref[...]
    activ, grad_gate, grad_up = gated(
        against_rows(gate_ref[...], tokens),
        against_rows(up_ref[...], tokens),
        against_rows(down_ref[...], grad_out),
    )
    activ_ref[...], grad_gate_ref[...], grad_up_ref[...] = activ, grad_gate, grad_up
    back = over_tokens(grad_gate, gate_ref[...]) + over_tokens(grad_up, up_ref[...])
    back, final = back.astype(bf16), over_tokens(activ, down_ref[...]).astype(bf16)

    @pl.when(step < steps // 2)
    def _():
        out_refs[0][...] = back
        out_refs[2][...] = final

    @pl.when(step >= steps // 2)
    def _():
        out_refs[1][...] = back
        out_refs[3][...] = final


def feed_forward(tokens, grad_out, own_gate, own_up, own_down):
    count, width = tokens.shape
    hidden = own_gate.shape[0]
    half, tile = count // 2, 512
    if not is_cube() or half % tile or width % 128 or hidden % 16:
        activ, grad_gate, grad_up = gated(
            against_rows(own_gate, tokens),
            against_rows(own_up, tokens),
            against_rows(own_down, grad_out),
        )
        back = over_tokens(grad_gate, own_gate) + over_tokens(grad_up, own_up)
        back, final = back.astype(bf16), over_tokens(activ, own_down).astype(bf16)
        return activ, grad_gate, grad_up, back[:half], back[half:], final[:half], final[half:]
    steps = count // tile
    rows = pl.BlockSpec((tile, width), lambda i: (i, 0))
    whole = pl.BlockSpec((hidden, width), lambda i: (0, 0))
    columns = pl.BlockSpec((hidden, tile), lambda i: (0, i))
    first = pl.BlockSpec((tile, width), lambda i: (jnp.minimum(i, steps // 2 - 1), 0))
    second = pl.BlockSpec((tile, width), lambda i: (jnp.maximum(i - steps // 2, 0), 0))
    return pl.pallas_call(
        feed_forward_kernel,
        grid=(steps,),
        in_specs=[rows, rows, whole, whole, whole],
        out_specs=[columns] * 3 + [first, second] * 2,
        out_shape=[jax.ShapeDtypeStruct((hidden, count), bf16)] * 3
        + [jax.ShapeDtypeStruct((half, width), bf16)] * 4,
        compiler_params=pltpu.CompilerParams(vmem_limit_bytes=40 << 20),
        cost_estimate=pl.CostEstimate(
            flops=12 * count * width * hidden,
            bytes_accessed=2 * (4 * count * width + 3 * hidden * (width + count)),
            transcendentals=count * hidden,
        ),
    )(tokens, grad_out, own_gate, own_up, own_down)


def per_device(inputs, norm_in, w_in, taps, w_out, norm_mid, w_gate, w_up, w_down, cotangent):
    micros, rows_held, width = inputs.shape
    peers = lax.axis_size("fsdp")
    reach = taps.shape[0] - 1
    owned = w_in.shape[0]
    hidden = w_down.shape[0]
    all_rows = micros * rows_held

    gate_up = [jnp.transpose(w).reshape(peers, hidden, owned) for w in (w_gate, w_up)]
    groups = lax.axis_size("dp")
    if groups % 2 == 0:
        one_way = (lax.axis_index("dp") & 1) == 0
        gate_up = jnp.where(one_way, gate_up[0], gate_up[1])
    else:
        gate_up = jnp.concatenate(gate_up, axis=1)
    grad_out = cotangent.reshape(all_rows, width)
    gate_up = exchange_early_cores(gate_up)
    in_x, in_y, w_out = together(*gather_sides(w_in), w_out)
    in_parts = gather_rest(w_in, in_x, in_y)
    out_x, out_y, in_parts[-1], gate_up = together(
        *gather_sides(w_out), in_parts[-1], gate_up
    )
    out_parts = gather_rest(w_out, out_x, out_y)
    grad_out_now, *gate_up = together(grad_out, *exchange_early_chips(gate_up))
    full_in = jnp.concatenate(in_parts, axis=0).reshape(width, 3 * width)
    smalls = jnp.concatenate([norm_in[None], norm_mid[None], taps], axis=0)
    smalls = jnp.pad(smalls, ((0, 8 - (reach + 3)), (0, 0)))
    smalls = jnp.transpose(gather(smalls)[:, : reach + 3], (1, 0, 2))
    smalls = relabel(smalls.reshape(reach + 3, width), back=True).astype(f32)
    gain_in, gain_mid, tap_values = smalls[0], smalls[1], smalls[2:]
    full_out = jnp.concatenate(out_parts, axis=0).reshape(width, width)
    grad_out_x, grad_out_y = gather_sides(grad_out_now)
    gate_up = jnp.transpose(exchanged_early(gate_up), (1, 0, 2)).reshape(-1, width)
    if groups % 2 == 0:
        other = along(gate_up, "dp", [(i, i ^ 1) for i in range(groups)])
        own_gate = jnp.where(one_way, gate_up, other)
        own_up = jnp.where(one_way, other, gate_up)
    else:
        own_gate, own_up = gate_up[:hidden], gate_up[hidden:]

    resid = inputs.reshape(all_rows, width).astype(f32)
    scale_in = inverse_rms(resid)
    normed_in = relabel((resid * scale_in * gain_in).astype(bf16))
    projected = times(normed_in, full_in)
    gate_b = projected[:, :width]
    gate_c = projected[:, width : 2 * width]
    values = projected[:, 2 * width :]
    mixed = (gate_b * values).astype(bf16).reshape(micros, rows_held, width)
    earlier = from_behind(mixed[:, rows_held - reach :], "fsdp", 1)
    extended = jnp.concatenate([earlier, mixed], axis=1).astype(f32)
    convolved = jnp.zeros((micros, rows_held, width), f32)
    for offset in range(reach + 1):
        convolved = convolved + tap_values[offset] * extended[:, offset : offset + rows_held]
    convolved = convolved.reshape(all_rows, width)
    gated = relabel((gate_c * convolved).astype(bf16))
    middle = resid + times(gated, full_out)
    scale_mid = inverse_rms(middle)
    normed_mid = (middle * scale_mid * gain_mid).astype(bf16)

    normed_mid, grad_out_x, grad_out_y = together(normed_mid, grad_out_x, grad_out_y)
    normed_all = gather(normed_mid).reshape(peers * all_rows, width)
    grad_out_all = jnp.concatenate(gather_rest(grad_out_now, grad_out_x, grad_out_y), axis=0)
    grad_out_all = grad_out_all.reshape(peers * all_rows, width)
    activ, grad_gate, grad_up, theirs, ours, final_theirs, final_ours = feed_forward(
        normed_all, grad_out_all, own_gate, own_up, w_down
    )
    near = scatter_near(theirs, ours)

    term_gate = times(grad_gate, normed_all).astype(bf16)
    came_gate = inward(term_gate)
    near, grad_up, activ, term_gate = together(near, grad_up, activ, term_gate)
    across = scatter_across(ours, near)
    grad_normed_mid = scattered(ours, near, scatter_last(ours, near, across))
    term_up = times(grad_up, normed_all).astype(bf16)
    term_down = times(activ, grad_out_all).astype(bf16)
    grad_normed_mid, term_up, term_down = together(grad_normed_mid, term_up, term_down)
    came_up = inward(term_up)
    pair_gate = add_pair(term_gate, came_gate)
    far_gate = between(pair_gate)

    back_mid, gain_mid_grad = norm_back(middle, scale_mid, gain_mid, grad_normed_mid)
    grad_middle = grad_out.astype(f32) + back_mid
    grad_branch = grad_middle.astype(bf16)
    grad_gated = relabel(against_rows(grad_branch, full_out), back=True)
    grad_c = grad_gated * convolved
    grad_conv = (grad_gated * gate_c).astype(bf16).reshape(micros, rows_held, width)
    later = from_behind(grad_conv[:, :reach], "fsdp", -1)
    ext_grad = jnp.concatenate([grad_conv, later], axis=1).astype(f32)
    grad_mixed = jnp.zeros((micros, rows_held, width), f32)
    tap_terms = []
    for offset in range(reach + 1):
        grad_mixed = (
            grad_mixed + tap_values[offset] * ext_grad[:, reach - offset : reach - offset + rows_held]
        )
        tap_terms.append(
            jnp.sum(extended[:, offset : offset + rows_held] * ext_grad[:, :rows_held], axis=(0, 1))
        )
    grad_mixed = grad_mixed.reshape(all_rows, width)
    grad_proj = [
        (grad_mixed * values).astype(bf16),
        grad_c.astype(bf16),
        (grad_mixed * gate_b).astype(bf16),
    ]

    half = width // 2
    normed_theirs, normed_ours = normed_in[:, :half], normed_in[:, half:]
    terms_out_c = [
        jnp.concatenate(
            [over_tokens(p, grad_branch).astype(bf16), over_tokens(q, grad_proj[1]).astype(bf16)],
            axis=1,
        )
        for p, q in ((gated[:, :half], normed_theirs), (gated[:, half:], normed_ours))
    ]
    near_out_c = scatter_near(*terms_out_c)
    near_out_c, grad_proj[0], grad_proj[2] = together(near_out_c, grad_proj[0], grad_proj[2])
    across_out_c = scatter_across(terms_out_c[1], near_out_c)
    grad_b_v = jnp.concatenate([grad_proj[0], grad_proj[2]], axis=1)
    terms_b_v = [over_tokens(p, grad_b_v).astype(bf16) for p in (normed_theirs, normed_ours)]
    grad_normed_in = relabel(
        against_rows(jnp.concatenate(grad_proj, axis=1), full_in), back=True
    )
    back_in, gain_in_grad = norm_back(resid, scale_in, gain_in, grad_normed_in)
    grad_inputs = (grad_middle + back_in).reshape(micros, rows_held, width)
    smalls = relabel(jnp.stack([gain_in_grad, gain_mid_grad] + tap_terms))
    smalls = jnp.pad(jnp.transpose(smalls), ((0, 0), (0, 128 - (reach + 3)))).astype(bf16)
    terms_b_v = [
        jnp.concatenate([terms_b_v[0], smalls[:half]], axis=1),
        jnp.concatenate([terms_b_v[1], smalls[half:]], axis=1),
    ]
    near_final = scatter_near(final_theirs, final_ours)
    across_out_c, *terms_b_v, far_gate, came_up, term_down, near_final = together(
        across_out_c, *terms_b_v, far_gate, came_up, term_down, near_final
    )

    total_gate = add_pair(pair_gate, far_gate)
    both = inward_outward(term_down, total_gate)
    pair_up = add_pair(term_up, came_up)
    far_up = between(pair_up)
    last_out_c = scatter_last(terms_out_c[1], near_out_c, across_out_c)
    near_b_v = scatter_near(*terms_b_v)
    across_b_v = scatter_across(terms_b_v[1], near_b_v)

    came_down, out_gate, far_up, across_b_v, *last_out_c = together(
        *both, far_up, across_b_v, *last_out_c
    )
    rows_out_c = scattered(terms_out_c[1], near_out_c, last_out_c).astype(bf16)
    came_out_c = inward(rows_out_c)
    pair_down = add_pair(term_down, came_down)
    far_down = between(pair_down)
    total_up = add_pair(pair_up, far_up)
    out_up = outward(total_up)
    last_b_v = scatter_last(terms_b_v[1], near_b_v, across_b_v)
    across_final = scatter_across(final_ours, near_final)

    came_out_c, out_up, far_down, across_final, *last_b_v = together(
        came_out_c, out_up, far_down, across_final, *last_b_v
    )
    rows_b_v = scattered(terms_b_v[1], near_b_v, last_b_v).astype(bf16)
    came_b_v = inward(rows_b_v)
    pair_out_c = add_pair(rows_out_c, came_out_c)
    far_out_c = between(pair_out_c)
    total_down = add_pair(pair_down, far_down)
    out_down = outward(total_down)
    mine = exchange_chips(
        jnp.concatenate(
            [
                jnp.transpose(settle(t, o).reshape(hidden, peers, owned), (1, 0, 2))
                for t, o in ((total_gate, out_gate), (total_up, out_up))
            ],
            axis=1,
        )
    )

    came_b_v, far_out_c, out_down, across_final, *mine = together(
        came_b_v, far_out_c, out_down, across_final, *mine
    )
    pair_b_v = add_pair(rows_b_v, came_b_v)
    far_b_v = between(pair_b_v)
    total_out_c = add_pair(pair_out_c, far_out_c)
    out_out_c = outward(total_out_c)
    last_final = scatter_last(final_ours, near_final, across_final)
    grad_w_down = settle(total_down, out_down).astype(f32)
    mine = exchange_cores(mine)
    by_rows = Layout(major_to_minor=(0, 1))
    grad_w_gate, grad_w_up = [
        with_layout_constraint(
            jnp.transpose(part.reshape(peers * hidden, owned)).astype(f32), by_rows
        )
        for part in (mine[:, :hidden], mine[:, hidden:])
    ]

    far_b_v, out_out_c, last_x, last_y, grad_w_down, grad_w_gate, grad_w_up = together(
        far_b_v, out_out_c, *last_final, grad_w_down, grad_w_gate, grad_w_up
    )
    total_b_v = add_pair(pair_b_v, far_b_v)
    out_b_v = outward(total_b_v)
    final = scattered(final_ours, near_final, (last_x, last_y))
    block_out = (middle + final).astype(bf16).reshape(micros, rows_held, width)
    out_b_v, block_out = together(out_b_v, block_out)
    total_out_c = settle(total_out_c, out_out_c).astype(f32)
    total_b_v = settle(total_b_v, out_b_v).astype(f32)
    grad_w_out = total_out_c[:, :width]
    grad_w_in = jnp.concatenate(
        [total_b_v[:, :width], total_out_c[:, width:], total_b_v[:, width : 2 * width]], axis=1
    )
    smalls = jnp.transpose(total_b_v[:, 2 * width : 2 * width + reach + 3])
    return (
        block_out,
        grad_inputs,
        smalls[0],
        grad_w_in,
        smalls[2:],
        grad_w_out,
        smalls[1],
        grad_w_gate,
        grad_w_up,
        grad_w_down,
    )


def solution(mesh):
    return jax.shard_map(
        per_device,
        mesh=mesh,
        in_specs=(
            P("dp", "fsdp", None),
            P("fsdp"),
            P("fsdp", None),
            P(None, "fsdp"),
            P("fsdp", None),
            P("fsdp"),
            P("fsdp", None),
            P("fsdp", None),
            P("fsdp", None),
            P("dp", "fsdp", None),
        ),
        out_specs=(
            P("dp", "fsdp", None),
            P("dp", "fsdp", None),
            P("fsdp"),
            P("fsdp", None),
            P(None, "fsdp"),
            P("fsdp", None),
            P("fsdp"),
            P("fsdp", None),
            P("fsdp", None),
            P("fsdp", None),
        ),
        check_vma=False,
    )
```
